512 devices in a mesh: band: 64 (over y_hi, z, core), helper: 8 (over y_lo, x).
Axes of the slice: x: 4, y: 4 (y_hi: 2, y_lo: 2; y = y_hi * 2 + y_lo), z: 16, core: 2. Of those that a mesh axis runs over, the one named last changes fastest.
Arguments:
- node_latent: bfloat16 [32768, 256], P(('band', 'helper')), may hold values from -6 to 6
- edge_latent: bfloat16 [524288, 256], P(('band', 'helper')), may hold values from -6 to 6
- grad_out_node: bfloat16 [32768, 256], P(('band', 'helper')), may hold values from -6 to 6
- grad_out_edge: bfloat16 [524288, 256], P(('band', 'helper')), may hold values from -6 to 6
- senders: int32 [524288], P(('band', 'helper')), may hold values from 0 to 767
- receivers: int32 [524288], P(('band', 'helper')), may hold values from 0 to 511, as said below
- band_edges: int32 [64], replicated, may hold values from 8 to 64, as said below
- halo_list: int32 [64, 128], P('band'), may hold values from 0 to 511, as said below
- sea_mask: int32 [32768], P(('band', 'helper')), may hold values 0 or 1
- edge_w1: bfloat16 [768, 256], replicated, may hold values from -0.21875 to 0.21875
- edge_b1: float32 [256], replicated, may hold values from -3 to 3
- edge_w2: bfloat16 [256, 256], replicated, may hold values from -0.375 to 0.375
- edge_b2: float32 [256], replicated, may hold values from -3 to 3
- node_w1: bfloat16 [512, 256], replicated, may hold values from -0.25 to 0.25
- node_b1: float32 [256], replicated, may hold values from -3 to 3
- node_w2: bfloat16 [256, 256], replicated, may hold values from -0.375 to 0.375
- node_b2: float32 [256], replicated, may hold values from -3 to 3
Outputs:
- grad_node: float32 [32768, 256], P(('band', 'helper'))
- grad_edge: bfloat16 [524288, 256], P(('band', 'helper'))
- grad_edge_w1: float32 [768, 256], replicated
- grad_edge_b1: float32 [256], replicated
- grad_edge_w2: float32 [256, 256], replicated
- grad_edge_b2: float32 [256], replicated
- grad_node_w1: float32 [512, 256], replicated
- grad_node_b1: float32 [256], replicated
- grad_node_w2: float32 [256, 256], replicated
- grad_node_b2: float32 [256], replicated
The draws below stay inside these ranges and needn't reach their ends.
Inputs may be any that keep to these rules, and one draw needn't show every extreme that they name: In every aligned block of 128 edge rows, all receivers lie in one aligned tile of 64 nodes. `band_edges`: A quarter of the bands, consecutive along the cycle, hold 64 live blocks; every other band holds between 8 and 24. `halo_list`: the 128 entries of a band are distinct.
All inputs are finite; a program needn't handle non-finite values. No bound on the sum of `sea_mask` on one device may be relied on, other than what follows from the above.
Results may differ from the reference program's by a relative error of at most 0.01.
Values may be sent and summed in bfloat16 or wider, within the bound.
A program may use at most 64 MiB of HBM per device.

```python
import math
import jax
import jax.numpy as jnp
from jax import lax

L = 256
NODE_DEV = 64
EB = 128
RTILE = 64
BLK_DEV = 8
NPB = 512
HALO = 128
NODES = 32768
EDGES = 524288
N_BAND = 64
N_HELPER = 8


def draw_receivers(key, part):
    block_count = EDGES // EB
    tiles = jax.random.randint(jax.random.fold_in(key, 11), (block_count, 1), 0, NPB // RTILE)
    lanes = jax.random.randint(jax.random.fold_in(key, 12), (block_count, EB), 0, RTILE)
    return (tiles * RTILE + lanes).reshape(EDGES).astype(jnp.int32)


def draw_band_edges(key, part):
    capacity = BLK_DEV * N_HELPER
    offset = jax.random.randint(jax.random.fold_in(key, 21), (), 0, N_BAND)
    band_ids = jnp.arange(N_BAND, dtype=jnp.int32)
    coastal = (band_ids - offset) % N_BAND < N_BAND // 4
    others = jax.random.randint(jax.random.fold_in(key, 22), (N_BAND,), capacity // 8, 3 * capacity // 8 + 1)
    return jnp.where(coastal, capacity, others).astype(jnp.int32)


def draw_halo_list(key, part):
    band_keys = jax.random.split(jax.random.fold_in(key, 31), N_BAND)

    def one_band(band_key):
        return jax.random.permutation(band_key, NPB)[:HALO]
    return jax.vmap(one_band)(band_keys).astype(jnp.int32)


def plant(values, stream_key, low, largest):
    longest = values.shape.index(max(values.shape))
    spots = []
    for shift in (0, 1):
        where = [jax.random.randint(jax.random.fold_in(stream_key, axis), (), 0, length) for axis, length in enumerate(values.shape)]
        where[longest] = (where[longest] + shift) % values.shape[longest]
        spots.append(tuple(where))
    return values.at[spots[0]].set(low).at[spots[1]].set(largest)


def level_of(key, dims, shards, smallest, largest):
    gain = 1.0
    for dim, blocks in shards:
        draws = jax.random.uniform(jax.random.fold_in(jax.random.fold_in(key, 6), dim), (blocks,), jnp.float32, smallest / len(shards), largest / len(shards))
        gain = gain * jnp.repeat(jnp.exp(draws), dims[dim] // blocks).reshape((-1,) + (1,) * (len(dims) - 1 - dim))
    return gain


def scatter_about(stream_key, extent, deviation, limit, pieces=(), held_as=jnp.bfloat16):
    loudness = level_of(stream_key, extent, pieces, -0.22, 0.18) if pieces else 1.0
    result = jax.random.normal(stream_key, extent, jnp.float32) * deviation * loudness
    return jnp.minimum(jnp.maximum(result, -limit), limit).astype(held_as)


def setup_inputs(seed: int = 0) -> dict:
    key_list = jax.random.split(jax.random.key(seed), 18)
    return {
        "node_latent": scatter_about(key_list[0], (NODES, L), 1.0, 6.0, ((0, 512),)),
        "edge_latent": scatter_about(key_list[1], (EDGES, L), 1.0, 6.0, ((0, 512),)),
        "grad_out_node": scatter_about(key_list[2], (NODES, L), 1.0, 6.0, ((0, 512),)),
        "grad_out_edge": scatter_about(key_list[3], (EDGES, L), 1.0, 6.0, ((0, 512),)),
        "senders": plant(jax.random.randint(key_list[4], (EDGES,), 0, NPB + 2 * HALO), jax.random.fold_in(key_list[4], 1), 0, (NPB + 2 * HALO) - 1).astype(jnp.int32),
        "receivers": draw_receivers(jax.random.fold_in(key_list[17], 71), 0),
        "band_edges": draw_band_edges(jax.random.fold_in(key_list[17], 71), 0),
        "halo_list": draw_halo_list(jax.random.fold_in(key_list[17], 71), 0),
        "sea_mask": plant((jax.random.randint(key_list[8], (NODES,), 0, 4) < 3).astype(jnp.int32), jax.random.fold_in(key_list[8], 1), 0, 1),
        "edge_w1": scatter_about(key_list[9], (3 * L, L), (3 * L) ** -0.5, 0.21875),
        "edge_b1": scatter_about(key_list[10], (L,), 0.5, 3.0, (), jnp.float32),
        "edge_w2": scatter_about(key_list[11], (L, L), L ** -0.5, 0.375),
        "edge_b2": scatter_about(key_list[12], (L,), 0.5, 3.0, (), jnp.float32),
        "node_w1": scatter_about(key_list[13], (2 * L, L), (2 * L) ** -0.5, 0.25),
        "node_b1": scatter_about(key_list[14], (L,), 0.5, 3.0, (), jnp.float32),
        "node_w2": scatter_about(key_list[15], (L, L), L ** -0.5, 0.375),
        "node_b2": scatter_about(key_list[16], (L,), 0.5, 3.0, (), jnp.float32),
    }


norm_eps = 1e-05

def layer_norm(pre_act):
    row_mean = lax.optimization_barrier(jnp.mean(pre_act, axis=-1, keepdims=True))
    centre = pre_act - row_mean
    inv_dev = lax.rsqrt(lax.optimization_barrier(jnp.mean(centre * centre, axis=-1, keepdims=True)) + norm_eps)
    return (centre * inv_dev, inv_dev)

def norm_back(grad_in, normed, inv_dev):
    return inv_dev * (grad_in - lax.optimization_barrier(jnp.mean(grad_in, axis=-1, keepdims=True)) - normed * lax.optimization_barrier(jnp.mean(grad_in * normed, axis=-1, keepdims=True)))

def silu_slope(pre_act):
    sigmoid_v = jax.nn.sigmoid(pre_act)
    return sigmoid_v * (1.0 + pre_act * (1.0 - sigmoid_v))

def dot_left_t(left_op, right_op):
    return lax.dot_general(left_op, right_op, (((0,), (0,)), ((), ())), preferred_element_type=jnp.float32)

def dot_right_t(left_op, right_op):
    return lax.dot_general(left_op, right_op, (((1,), (1,)), ((), ())), preferred_element_type=jnp.float32)

def mlp_forward(inputs, w_first, b_first, w_second, b_second):
    pre_act = jnp.dot(inputs, w_first, preferred_element_type=jnp.float32) + b_first
    hidden = jax.nn.silu(pre_act).astype(jnp.bfloat16)
    normed, inv_dev = layer_norm(jnp.dot(hidden, w_second, preferred_element_type=jnp.float32) + b_second)
    return (pre_act, hidden, normed, inv_dev)

def mlp_backward(inputs, w_first, w_second, pre_act, hidden, normed, inv_dev, grad_out):
    grad_second = norm_back(grad_out, normed, inv_dev)
    second_b = grad_second.astype(jnp.bfloat16)
    gw_second = dot_left_t(hidden, second_b)
    gb_second = lax.optimization_barrier(jnp.sum(grad_second, axis=0))
    grad_first = dot_right_t(second_b, w_second) * silu_slope(pre_act)
    first_b = grad_first.astype(jnp.bfloat16)
    gw_first = dot_left_t(inputs, first_b)
    gb_first = lax.optimization_barrier(jnp.sum(grad_first, axis=0))
    grad_inputs = dot_right_t(first_b, w_first)
    return (grad_inputs, gw_first, gb_first, gw_second, gb_second)

def reference(node_latent, edge_latent, grad_out_node, grad_out_edge, senders, receivers, band_edges, halo_list, sea_mask, edge_w1, edge_b1, edge_w2, edge_b2, node_w1, node_b1, node_w2, node_b2):
    band_size = NODE_DEV * N_HELPER
    features = L
    per_band = N_HELPER * BLK_DEV * EB
    nodes = node_latent.reshape(N_BAND, band_size, features)

    def pick_rows(band_nodes, halo_ids):
        return band_nodes[halo_ids]
    halo_rows = jax.vmap(pick_rows)(nodes, halo_list)
    lookups = jnp.concatenate([nodes, jnp.roll(halo_rows, 1, axis=0), jnp.roll(halo_rows, -1, axis=0)], axis=1)
    slot_ids = jnp.arange(BLK_DEV, dtype=jnp.int32)[None, :] * N_HELPER + jnp.arange(N_HELPER, dtype=jnp.int32)[:, None]
    alive_mask = (slot_ids[None, :, :] < band_edges[:, None, None]).astype(jnp.float32)
    alive_mask = jnp.broadcast_to(alive_mask[..., None], (N_BAND, N_HELPER, BLK_DEV, EB)).reshape(N_BAND, per_band)

    def one_band(band_item):
        lookup, band_nodes, edge_rows, grad_edges, send_ids, recv_ids, alive, grad_rows, sea_rows = band_item
        inputs = jnp.concatenate([lookup[send_ids], band_nodes[recv_ids], edge_rows], axis=1)
        pre_act, hidden, normed, inv_dev = mlp_forward(inputs, edge_w1, edge_b1, edge_w2, edge_b2)
        message = lax.optimization_barrier(normed.astype(jnp.bfloat16)).astype(jnp.float32) * alive[:, None]
        agg_rows = jax.ops.segment_sum(message, recv_ids, num_segments=band_size)
        node_in = jnp.concatenate([band_nodes, agg_rows.astype(jnp.bfloat16)], axis=1)
        n_pre, n_hidden, n_normed, n_inv = mlp_forward(node_in, node_w1, node_b1, node_w2, node_b2)
        node_seed = sea_rows[:, None].astype(jnp.float32) * grad_rows.astype(jnp.float32)
        node_back = mlp_backward(node_in, node_w1, node_w2, n_pre, n_hidden, n_normed, n_inv, node_seed)
        agg_grad = lax.optimization_barrier(node_back[0][:, features:].astype(jnp.bfloat16))
        msg_grad = (grad_edges.astype(jnp.float32) + agg_grad[recv_ids].astype(jnp.float32)) * alive[:, None]
        edge_back = mlp_backward(inputs, edge_w1, edge_w2, pre_act, hidden, normed, inv_dev, msg_grad)
        grad_inputs = edge_back[0]
        lookup_grad = jnp.zeros((band_size + 2 * HALO, features), jnp.float32)
        lookup_grad = lookup_grad.at[send_ids].add(grad_inputs[:, :features])
        lookup_grad = lookup_grad.at[recv_ids].add(grad_inputs[:, features:2 * features])
        edge_grad = ((grad_edges.astype(jnp.float32) + grad_inputs[:, 2 * features:]) * alive[:, None]).astype(jnp.bfloat16)
        node_grad = grad_rows.astype(jnp.float32) + node_back[0][:, :features]
        return (lookup_grad, edge_grad, node_grad, edge_back[1:], node_back[1:])
    band_items = (lookups, nodes, edge_latent.reshape(N_BAND, per_band, features), grad_out_edge.reshape(N_BAND, per_band, features), senders.reshape(N_BAND, per_band), receivers.reshape(N_BAND, per_band), alive_mask, grad_out_node.reshape(N_BAND, band_size, features), sea_mask.reshape(N_BAND, band_size))
    lookup_grads, edge_grads, node_grads, edge_wgrads, node_wgrads = lax.map(one_band, band_items)
    returned = jnp.roll(lookup_grads[:, band_size:band_size + HALO], -1, axis=0) + jnp.roll(lookup_grads[:, band_size + HALO:], 1, axis=0)
    node_grads = node_grads + lookup_grads[:, :band_size]

    def add_back(band_nodes, halo_ids, extra_rows):
        return band_nodes.at[halo_ids].add(extra_rows)
    node_grads = jax.vmap(add_back)(node_grads, halo_list, returned)
    edge_scale = 1.0 / math.sqrt(EDGES)
    node_scale = 1.0 / math.sqrt(NODES)
    ew = [lax.optimization_barrier(jnp.sum(grad_part, axis=0)) * edge_scale for grad_part in edge_wgrads]
    nw = [lax.optimization_barrier(jnp.sum(grad_part, axis=0)) * node_scale for grad_part in node_wgrads]
    return (node_grads.reshape(NODES, features), edge_grads.reshape(EDGES, features), ew[0], ew[1], ew[2], ew[3], nw[0], nw[1], nw[2], nw[3])
```

```python
import functools
import math
from types import SimpleNamespace

import jax
import jax.numpy as jnp
from jax import lax
from jax.experimental import pallas as pl
from jax.experimental.pallas import tpu as pltpu
from jax.sharding import PartitionSpec as P

Y_HI = 2
Y_LO = 2
Z_HI = 4
Z_LO = 4
CORES = 2
EB = 128
EARLY = 3
ROWS = 256
LANES = 128
VMEM_BYTES = 56 * 1024 * 1024

norm_eps = 1e-05
F32 = jnp.float32
BF16 = jnp.bfloat16
MESH = pl.DeviceIdType.MESH


def dot(a, b):
    return jnp.dot(a, b, preferred_element_type=F32)


def dot_nt(a, b):
    return lax.dot_general(a, b, (((1,), (1,)), ((), ())), preferred_element_type=F32)


def layer_norm(pre_act):
    row_mean = jnp.mean(pre_act, axis=-1, keepdims=True)
    centre = pre_act - row_mean
    inv_dev = lax.rsqrt(jnp.mean(centre * centre, axis=-1, keepdims=True) + norm_eps)
    return centre * inv_dev, inv_dev


def norm_back(grad_in, normed, inv_dev):
    return inv_dev * (
        grad_in
        - jnp.mean(grad_in, axis=-1, keepdims=True)
        - normed * jnp.mean(grad_in * normed, axis=-1, keepdims=True)
    )


def column(row):
    n = row.shape[1]
    diag = lax.broadcasted_iota(jnp.int32, (n, n), 0) == lax.broadcasted_iota(jnp.int32, (n, n), 1)
    return jnp.sum(jnp.where(diag, row, 0.0), axis=1, keepdims=True)


def onehot_cols(col, width):
    ids = lax.broadcasted_iota(jnp.int32, (col.shape[0], width), 1).astype(F32)
    return jnp.where(ids == col, 1.0, 0.0).astype(BF16)


def onehot_rows(row, height):
    ids = lax.broadcasted_iota(jnp.int32, (height, row.shape[1]), 0).astype(F32)
    return jnp.where(ids == row, 1.0, 0.0).astype(BF16)


def at(index, size):
    return pl.ds(pl.multiple_of(index * size, size), size)


def loop(count, body):
    if count == 1:
        body(0)
        return

    def step(i, carry):
        body(i)
        return carry

    lax.fori_loop(0, count, step, 0)


class Flow:
    def __init__(self, flows, send_sem, recv_sem, sent, landed):
        self.send_sem, self.recv_sem, self.sent, self.landed = send_sem, recv_sem, sent, landed
        self.arrived = False
        flows.append(self)

    def send(self, src, dst, device):
        pltpu.make_async_remote_copy(
            src_ref=src,
            dst_ref=dst,
            send_sem=self.send_sem,
            recv_sem=self.recv_sem,
            device_id=device,
            device_id_type=MESH,
        ).start()

    def wait(self):
        self.arrived = True
        pltpu.make_async_copy(self.landed, self.landed, self.recv_sem).wait()

    def drain(self):
        if not self.arrived:
            self.wait()
        pltpu.make_async_copy(self.sent, self.sent, self.send_sem).wait()


class Local:
    def __init__(self, flows, src, dst, sem):
        self.copy = pltpu.make_async_copy(src, dst, sem)
        self.copy.start()
        self.arrived = False
        flows.append(self)

    def wait(self):
        self.arrived = True
        self.copy.wait()

    def drain(self):
        if not self.arrived:
            self.wait()


def kernel(dims, names, *refs):
    flows = []
    r = SimpleNamespace(**dict(zip(names, refs)))
    r.n = SimpleNamespace(out=r.n_out, land=r.n_land, z_lo=r.n_z_lo, z_hi=r.n_z_hi, full=r.n_full, s=r.n_s, r=r.n_r)
    r.e = SimpleNamespace(out=r.e_out, land=r.e_land, z_lo=r.e_z_lo, z_hi=r.e_z_hi, full=r.e_full, s=r.e_s, r=r.e_r)
    steps(dims, r, flows)
    for flow in flows:
        flow.drain()


def steps(dims, r, flows):
    H, E, N, HALO, L, G = dims.H, dims.E, dims.N, dims.HALO, dims.L, dims.G
    BAND = N * H
    LOOK = BAND + 2 * HALO
    ALL = LOOK + BAND
    NBLK = E // ROWS
    ZN = Z_HI * Z_LO

    band = lax.axis_index("band")
    helper = lax.axis_index("helper")
    n_band = Y_HI * ZN * CORES
    core = lax.rem(band, CORES)
    z = lax.rem(lax.div(band, CORES), ZN)
    y_hi = lax.div(band, CORES * ZN)
    z_lo = lax.rem(z, Z_LO)
    z_hi = lax.div(z, Z_LO)
    plane = y_hi * CORES + core
    me = plane * H + helper
    X = H // Y_LO
    x, y = lax.rem(helper, X), y_hi * Y_LO + lax.div(helper, X)
    KINDS = 4
    kind_own = lax.rem(x + y + 2 * core, KINDS)

    def owner(kind, j):
        to_y, to_core = lax.rem(y + j // CORES, Y_HI * Y_LO), lax.rem(core + j % CORES, CORES)
        to_x = lax.rem(kind + 2 * KINDS - to_y - 2 * to_core, KINDS)
        to_plane = lax.div(to_y, Y_LO) * CORES + to_core
        to_helper = lax.rem(to_y, Y_LO) * X + to_x
        return to_plane * H + to_helper, (to_core * KINDS + kind) * (Y_HI * Y_LO) + to_y, place(to_plane, z, to_helper)

    def place(plane_i, z_i, helper_i):
        return dict(
            band=(lax.div(plane_i, CORES) * ZN + z_i) * CORES + lax.rem(plane_i, CORES),
            helper=helper_i,
        )

    def in_group(k):
        g = lax.rem(me + k, G)
        return g, place(lax.div(g, H), z, lax.rem(g, H))

    def in_helper(k):
        return dict(band=band, helper=lax.rem(helper + k, H))

    def in_plane(k):
        return place(lax.rem(plane + k, Y_HI * CORES), z, helper)

    def in_z_lo(k):
        return place(plane, z_hi * Z_LO + lax.rem(z_lo + k, Z_LO), helper)

    def in_z_hi(k):
        return place(plane, lax.rem(z_hi + k, Z_HI) * Z_LO + z_lo, helper)

    next_band = dict(band=lax.rem(band + 1, n_band), helper=helper)
    prev_band = dict(band=lax.rem(band + n_band - 1, n_band), helper=helper)

    def flow(i, sent, landed):
        return Flow(flows, r.s_sem.at[i], r.r_sem.at[i], sent, landed)

    load_edge = Local(flows, r.edge_hbm, r.edge, r.load_sem.at[0])
    load_grad = Local(flows, r.gedge_hbm, r.gedge, r.load_sem.at[1])

    barrier = pltpu.get_barrier_semaphore()

    def greet(device):
        pl.semaphore_signal(barrier, inc=1, device_id=device, device_id_type=MESH)

    for k in range(1, G):
        greet(in_group(k)[1])
    for k in range(1, Z_LO):
        greet(in_z_lo(k))
    for k in range(1, Z_HI):
        greet(in_z_hi(k))
    greet(next_band)
    greet(prev_band)
    hot, hot_t = r.hot, r.hot_t

    def block_onehots(j):
        rows = at(j, EB)
        s_row, r_row = r.send_ids[pl.ds(j, 1), :].astype(F32), r.recv_ids[pl.ds(j, 1), :].astype(F32)
        hot[rows, :LOOK] = onehot_cols(column(s_row), LOOK)
        hot[rows, LOOK:] = onehot_cols(column(r_row), BAND)
        hot_t[:LOOK, rows] = onehot_rows(s_row, LOOK)
        hot_t[LOOK:, rows] = onehot_rows(r_row, BAND)

    loop(EARLY, block_onehots)
    pl.semaphore_wait(barrier, G - 1 + Z_LO - 1 + Z_HI - 1 + 2)

    look, proj = r.look, r.proj
    others = look.at[pl.ds(0, (H - 1) * N)]
    rows_flow = flow(0, others, others)
    for k in range(1, H):
        rows_flow.send(r.node, look.at[at(helper, N)], in_helper(k))
    look[at(helper, N), :] = r.node[...]


    loop(E // EB - EARLY, lambda j: block_onehots(j + EARLY))
    halo_row = r.halo[...].astype(F32)
    halo_t = onehot_rows(halo_row, BAND)
    r.halo_t[:, :HALO] = halo_t
    r.halo_t[:, HALO:] = halo_t
    sea = column(r.sea[...].astype(F32))

    live_blocks = r.band_edges[band]
    slot = lax.shift_right_logical(lax.broadcasted_iota(jnp.int32, (E, 1), 0), int(math.log2(EB)))
    r.live[...] = jnp.where(slot * H + helper < live_blocks, 1.0, 0.0)

    load_edge.wait()
    edge, pre = r.edge, r.pre

    def edge_part(i):
        rows = at(i, ROWS)
        block = edge[rows, :]
        pre[rows, :] = dot(block, r.ew1[2 * L :, :]) + r.eb1[...]
        r.edge_t[:, rows] = block.T

    loop(NBLK, edge_part)

    rows_flow.wait()
    r.halo_out[...] = dot(onehot_cols(column(halo_row), BAND), look[:BAND, :]).astype(BF16)
    from_prev, from_next = look.at[pl.ds(BAND, HALO)], look.at[pl.ds(BAND + HALO, HALO)]
    halo_up = flow(1, r.halo_out, from_prev)
    halo_down = flow(2, r.halo_out, from_next)
    halo_up.send(r.halo_out, from_prev, next_band)
    halo_down.send(r.halo_out, from_next, prev_band)

    def project(i):
        rows = at(i, EB)
        block = look[rows, :]
        proj[rows, :] = dot(block, r.ew1[:L, :]).astype(BF16)
        proj[pl.ds(pl.multiple_of(LOOK + i * EB, EB), EB), :] = dot(block, r.ew1[L : 2 * L, :]).astype(BF16)

    loop(BAND // EB, project)

    def own_part(i):
        rows = at(i, ROWS)
        pre[rows, :] += dot(hot[rows, :BAND], proj[:BAND, :]) + dot(hot[rows, LOOK:], proj[LOOK:, :])

    loop(NBLK, own_part)
    halo_up.wait()
    halo_down.wait()
    proj[BAND:LOOK, :] = dot(look[BAND:, :], r.ew1[:L, :]).astype(BF16)

    hidden, normed, inv, msg = r.hidden, r.normed, r.inv, r.msg

    def edge_forward(i):
        rows = at(i, ROWS)
        pre_act = pre[rows, :] + dot(hot[rows, BAND:LOOK], proj[BAND:LOOK, :])
        sig = jax.nn.sigmoid(pre_act)
        hid = (pre_act * sig).astype(BF16)
        hidden[rows, :] = hid
        pre[rows, :] = sig * (1.0 + pre_act * (1.0 - sig))
        norm, inv_dev = layer_norm(dot(hid, r.ew2[...]) + r.eb2[...])
        normed[rows, :] = norm
        inv[rows, :] = inv_dev
        msg[rows, :] = (norm * r.live[rows, :]).astype(BF16)

    loop(NBLK, edge_forward)

    agg_out, agg_in = r.agg_out, r.agg_in

    def sum_messages(i):
        agg_out[at(i, EB), :] = dot(hot_t[pl.ds(pl.multiple_of(LOOK + i * EB, EB), EB), :], msg[...]).astype(BF16)

    loop(BAND // EB, sum_messages)
    agg_flow = flow(3, others, agg_in)
    for k in range(1, H):
        to = in_helper(k)
        agg_flow.send(agg_out.at[at(lax.rem(helper + k, H), N)], agg_in.at[pl.ds((k - 1) * N, N)], to)

    def hidden_turn(i):
        rows = at(i, ROWS)
        r.hidden_t[:, rows] = hidden[rows, :].T

    def look_turn(i):
        rows = at(i, EB)
        r.look_t[:, rows] = look[rows, :].T

    loop(NBLK, hidden_turn)
    loop(LOOK // EB, look_turn)
    agg_flow.wait()
    agg = agg_out[at(helper, N), :].astype(F32)
    for k in range(H - 1):
        agg += agg_in[k * N : (k + 1) * N, :].astype(F32)
    agg = agg.astype(BF16)

    node = r.node[...]
    nw1 = r.nw1
    n_pre = dot(node, nw1[:L, :]) + dot(agg, nw1[L:, :]) + r.nb1[...]
    n_sig = jax.nn.sigmoid(n_pre)
    n_hid = (n_pre * n_sig).astype(BF16)
    n_norm, n_inv = layer_norm(dot(n_hid, r.nw2[...]) + r.nb2[...])
    g_node = r.gnode[...].astype(F32)
    n_dz = norm_back(sea * g_node, n_norm, n_inv)
    n_dz_b = n_dz.astype(BF16)
    n_dpre = dot_nt(n_dz_b, r.nw2[...]) * (n_sig * (1.0 + n_pre * (1.0 - n_sig)))
    n_dpre_b = n_dpre.astype(BF16)
    agg_grad = r.agg_grad
    mine = agg_grad.at[at(helper, N)]
    agg_grad[at(helper, N), :] = dot_nt(n_dpre_b, nw1[L:, :]).astype(BF16)
    back_flow = flow(4, others, agg_grad.at[pl.ds(0, (H - 1) * N)])
    for k in range(1, H):
        back_flow.send(mine, mine, in_helper(k))

    own = (core * KINDS + kind_own) * (Y_HI * Y_LO) + y
    node_sums = Reduced(flows, r.n, dims, me, me, z_lo, z_hi, in_group, in_z_lo, in_z_hi)
    edge_sums = Reduced(flows, r.e, dims, me, own, z_lo, z_hi, in_group, in_z_lo, in_z_hi)

    bias_axes = (
        (r.bias0, H, helper, in_helper),
        (r.bias1, Y_HI * CORES, plane, in_plane),
        (r.bias2, Z_LO, z_lo, in_z_lo),
        (r.bias3, Z_HI, z_hi, in_z_hi),
    )

    def bias_send(step):
        ref, count, slot_i, device_of = bias_axes[step]
        mine = ref.at[slot_i]
        rest = ref.at[pl.ds(0, count - 1)]
        bias_flow = Flow(flows, r.bias_s.at[step], r.bias_r.at[step], rest, rest)
        for k in range(1, count):
            bias_flow.send(mine, mine, device_of(k))
        return bias_flow

    def bias_sum(step, bias_flow):
        ref, count = bias_axes[step][:2]
        bias_flow.wait()
        total = ref[0]
        for k in range(1, count):
            total += ref[k]
        return total

    node_sums.put(0, dot(node.T, n_dpre_b))
    node_sums.put(L, dot(agg.T, n_dpre_b))
    node_sums.put(2 * L, dot(n_hid.T, n_dz_b))
    node_sums.scatter()
    node_din = g_node + dot_nt(n_dpre_b, nw1[:L, :])

    load_grad.wait()
    gedge, dz_b, dpre_b = r.gedge, r.dz_b, r.dpre_b
    back_flow.wait()

    def edge_back(i, sums):
        rows = at(i, ROWS)
        grad = gedge[rows, :].astype(F32) + dot(hot[rows, LOOK:], agg_grad[...])
        dz = norm_back(grad * r.live[rows, :], normed[rows, :], inv[rows, :])
        second = dz.astype(BF16)
        dz_b[rows, :] = second
        dpre = dot_nt(second, r.ew2[...]) * pre[rows, :]
        dpre_b[rows, :] = dpre.astype(BF16)
        return sums[0] + jnp.sum(dpre, axis=0, keepdims=True), sums[1] + jnp.sum(dz, axis=0, keepdims=True)

    zero = jnp.zeros((1, L), F32)
    e_gb1, e_gb2 = lax.fori_loop(0, NBLK, edge_back, (zero, zero))

    scat = r.scat

    def scatter(i):
        rows = at(i, ROWS)
        scat[rows, :] = dot(hot_t[rows, :], dpre_b[...]).astype(BF16)

    edge_sums.put(3 * L, dot(r.hidden_t[...], dz_b[...]))
    edge_sums.scatter_kind(3, owner)
    edge_sums.put(2 * L, dot(r.edge_t[...], dpre_b[...]))
    edge_sums.scatter_kind(2, owner)
    loop(BAND // ROWS, lambda i: scatter(LOOK // ROWS + i))
    edge_sums.put(L, dot(r.look_t[:, :BAND], scat[LOOK:, :]))
    edge_sums.scatter_kind(1, owner)
    loop(LOOK // ROWS, scatter)
    edge_sums.put(0, dot(r.look_t[...], scat[:LOOK, :]))
    edge_sums.scatter_kind(0, owner)
    node_sums.along_z_lo()

    tiles = (e_gb1, e_gb2, jnp.sum(n_dpre, axis=0, keepdims=True), jnp.sum(n_dz, axis=0, keepdims=True))
    for i, row in enumerate(tiles):
        r.bias0[helper, 2 * i : 2 * i + 1, :] = row[:, :LANES]
        r.bias0[helper, 2 * i + 1 : 2 * i + 2, :] = row[:, LANES:]
    bias_flow = bias_send(0)

    halo_back, halo_in = r.halo_back, r.halo_in
    halo_back[...] = dot_nt(scat[BAND:LOOK, :], r.ew1[:L, :]).astype(BF16)
    upper, lower = pl.ds(0, HALO), pl.ds(HALO, HALO)
    back_down = flow(5, halo_back.at[upper], halo_in.at[upper])
    back_up = flow(6, halo_back.at[lower], halo_in.at[lower])
    back_down.send(halo_back.at[upper], halo_in.at[upper], prev_band)
    back_up.send(halo_back.at[lower], halo_in.at[lower], next_band)

    node_sums.along_z_hi()

    band_grad = r.band_grad
    band_grad[...] = dot_nt(scat[:BAND, :], r.ew1[:L, :]) + dot_nt(scat[LOOK:, :], r.ew1[L : 2 * L, :])

    r.bias1[plane] = bias_sum(0, bias_flow)
    bias_flow = bias_send(1)
    edge_sums.along_z_lo()

    node_sums.gather()

    r.bias2[z_lo] = bias_sum(1, bias_flow)
    bias_flow = bias_send(2)
    edge_sums.along_z_hi()

    back_down.wait()
    back_up.wait()
    node_out, node_in = r.node_out, r.node_in
    node_out[...] = (band_grad[...] + dot(r.halo_t[...], halo_in[...])).astype(BF16)
    node_flow = flow(7, others, node_in)
    for k in range(1, H):
        to = in_helper(k)
        node_flow.send(node_out.at[at(lax.rem(helper + k, H), N)], node_in.at[pl.ds((k - 1) * N, N)], to)

    def edge_grad(i):
        rows = at(i, ROWS)
        din = dot_nt(dpre_b[rows, :], r.ew1[2 * L :, :])
        r.edge_new[rows, :] = ((gedge[rows, :].astype(F32) + din) * r.live[rows, :]).astype(BF16)

    loop(NBLK, edge_grad)
    Local(flows, r.edge_new, r.o_edge, r.load_sem.at[2])

    r.bias3[z_hi] = bias_sum(2, bias_flow)
    bias_flow = bias_send(3)
    edge_sums.gather()

    node_flow.wait()
    total = node_out[at(helper, N), :].astype(F32)
    for k in range(H - 1):
        total += node_in[k * N : (k + 1) * N, :].astype(F32)
    r.o_node[...] = total + node_din
    r.o_bias[...] = bias_sum(3, bias_flow)
    node_sums.done.wait()
    edge_sums.done.wait()


class Reduced:
    def __init__(self, flows, refs, dims, me, own, z_lo, z_hi, in_group, in_z_lo, in_z_hi):
        self.flows, self.refs, self.me, self.own, self.z_lo, self.z_hi = flows, refs, me, own, z_lo, z_hi
        self.in_group, self.in_z_lo, self.in_z_hi = in_group, in_z_lo, in_z_hi
        self.G = dims.G
        self.piece = refs.out.shape[0] // dims.G
        rest = pl.ds(0, (self.G - 1) * self.piece)
        self.first = self.flow(0, refs.out.at[rest], refs.land.at[rest])

    def flow(self, i, sent, landed):
        return Flow(self.flows, self.refs.s.at[i], self.refs.r.at[i], sent, landed)

    def put(self, first, value):
        out = self.refs.out
        half, count = out.shape[0] // 2, value.shape[0]
        out[first : first + count, :] = value[:, :LANES].astype(BF16)
        out[half + first : half + first + count, :] = value[:, LANES:].astype(BF16)

    def scatter_to(self, g, piece_i, device):
        piece = self.piece
        self.first.send(self.refs.out.at[at(piece_i, piece)], self.refs.land.at[at(self.me, piece)], device)

    def scatter(self):
        for k in range(1, self.G):
            g, to = self.in_group(k)
            self.scatter_to(g, g, to)

    def scatter_kind(self, kind, owner):
        for j in range(self.G // 4):
            g, piece_i, to = owner(kind, j)

            @pl.when(g != self.me)
            def _():
                self.scatter_to(g, piece_i, to)

    def along_z_lo(self):
        out, land, quad, piece = self.refs.out, self.refs.land, self.refs.z_lo, self.piece
        self.first.wait()
        land[at(self.me, piece), :] = out[at(self.own, piece), :]
        zero = jnp.zeros((piece, LANES), F32)
        total = lax.fori_loop(0, self.G, lambda k, acc: acc + land[at(k, piece), :].astype(F32), zero)
        mine = quad.at[self.z_lo]
        quad[self.z_lo] = total.astype(BF16)
        rest = quad.at[pl.ds(0, Z_LO - 1)]
        self.second = self.flow(1, rest, rest)
        for k in range(1, Z_LO):
            self.second.send(mine, mine, self.in_z_lo(k))

    def along_z_hi(self):
        old, quad = self.refs.z_lo, self.refs.z_hi
        self.second.wait()
        total = old[0].astype(F32)
        for k in range(1, Z_LO):
            total += old[k].astype(F32)
        mine = quad.at[self.z_hi]
        quad[self.z_hi] = total.astype(BF16)
        rest = quad.at[pl.ds(0, Z_HI - 1)]
        self.third = self.flow(2, rest, rest)
        for k in range(1, Z_HI):
            self.third.send(mine, mine, self.in_z_hi(k))

    def gather(self):
        quad, full, piece = self.refs.z_hi, self.refs.full, self.piece
        self.third.wait()
        total = quad[0].astype(F32)
        for k in range(1, Z_HI):
            total += quad[k].astype(F32)
        mine = full.at[at(self.own, piece)]
        full[at(self.own, piece), :] = total.astype(BF16)
        rest = full.at[pl.ds(0, (self.G - 1) * piece)]
        self.done = self.flow(3, rest, rest)
        for k in range(1, self.G):
            self.done.send(mine, mine, self.in_group(k)[1])


def finish(dims, node_hbm, edge_hbm, node_sums_hbm, edge_sums_hbm, bias_hbm, o_node, o_edge, *rest):
    o_ew1, o_eb1, o_ew2, o_eb2, o_nw1, o_nb1, o_nw2, o_nb2, node_sums, edge_sums, bias, sems = rest
    pairs = (
        (edge_sums_hbm, edge_sums),
        (node_sums_hbm, node_sums),
        (bias_hbm, bias),
        (edge_hbm, o_edge),
        (node_hbm, o_node),
    )
    copies = [pltpu.make_async_copy(src, dst, sems.at[i]) for i, (src, dst) in enumerate(pairs)]
    for copy in copies:
        copy.start()

    def weights(full, targets, scale):
        half, first = full.shape[0] // 2, 0
        for out in targets:
            count = out.shape[0]
            out[:, :LANES] = full[first : first + count, :].astype(F32) * scale
            out[:, LANES:] = full[half + first : half + first + count, :].astype(F32) * scale
            first += count

    copies[0].wait()
    weights(edge_sums, (o_ew1, o_ew2), dims.edge_scale)
    copies[1].wait()
    weights(node_sums, (o_nw1, o_nw2), dims.node_scale)
    copies[2].wait()
    for i, (out, scale) in enumerate(
        ((o_eb1, dims.edge_scale), (o_eb2, dims.edge_scale), (o_nb1, dims.node_scale), (o_nb2, dims.node_scale))
    ):
        out[:, :LANES] = bias[2 * i : 2 * i + 1, :] * scale
        out[:, LANES:] = bias[2 * i + 1 : 2 * i + 2, :] * scale
    copies[3].wait()
    copies[4].wait()


def on_device(
    node_latent,
    edge_latent,
    grad_out_node,
    grad_out_edge,
    senders,
    receivers,
    band_edges,
    halo_list,
    sea_mask,
    edge_w1,
    edge_b1,
    edge_w2,
    edge_b2,
    node_w1,
    node_b1,
    node_w2,
    node_b2,
):
    H = lax.axis_size("helper")
    bands = lax.axis_size("band")
    N, L = node_latent.shape
    E = edge_latent.shape[0]
    HALO = halo_list.shape[1]
    BAND = N * H
    LOOK = BAND + 2 * HALO
    ALL = LOOK + BAND
    G = H * Y_HI * CORES
    dims = SimpleNamespace(
        H=H,
        E=E,
        N=N,
        HALO=HALO,
        L=L,
        G=G,
        edge_scale=1.0 / math.sqrt(E * H * bands),
        node_scale=1.0 / math.sqrt(N * H * bands),
    )
    V, S, ANY = pltpu.VMEM, pltpu.SMEM, pl.ANY
    inputs = dict(
        node=(node_latent, V),
        edge_hbm=(edge_latent, ANY),
        gnode=(grad_out_node, V),
        gedge_hbm=(grad_out_edge, ANY),
        send_ids=(senders.reshape(E // EB, EB), V),
        recv_ids=(receivers.reshape(E // EB, EB), V),
        band_edges=(band_edges, S),
        halo=(halo_list, V),
        sea=(sea_mask.reshape(1, N), V),
        ew1=(edge_w1, V),
        eb1=(edge_b1.reshape(1, L), V),
        ew2=(edge_w2, V),
        eb2=(edge_b2.reshape(1, L), V),
        nw1=(node_w1, V),
        nb1=(node_b1.reshape(1, L), V),
        nw2=(node_w2, V),
        nb2=(node_b2.reshape(1, L), V),
    )
    n_rows, e_rows = 3 * L * (L // LANES), 4 * L * (L // LANES)
    outputs = dict(
        o_node=((N, L), F32, V),
        o_edge=((E, L), BF16, ANY),
        n_full=((n_rows, LANES), BF16, V),
        e_full=((e_rows, LANES), BF16, V),
        o_bias=((8, LANES), F32, V),
    )
    scratch = dict(
        edge=V((E, L), BF16),
        gedge=V((E, L), BF16),
        edge_new=V((E, L), BF16),
        look=V((LOOK, L), BF16),
        look_t=V((L, LOOK), BF16),
        edge_t=V((L, E), BF16),
        hidden_t=V((L, E), BF16),
        proj=V((ALL, L), BF16),
        hot=V((E, ALL), BF16),
        hot_t=V((ALL, E), BF16),
        halo_t=V((BAND, 2 * HALO), BF16),
        halo_out=V((HALO, L), BF16),
        halo_back=V((2 * HALO, L), BF16),
        halo_in=V((2 * HALO, L), BF16),
        live=V((E, 1), F32),
        pre=V((E, L), F32),
        hidden=V((E, L), BF16),
        normed=V((E, L), F32),
        inv=V((E, 1), F32),
        msg=V((E, L), BF16),
        dz_b=V((E, L), BF16),
        dpre_b=V((E, L), BF16),
        agg_out=V((BAND, L), BF16),
        agg_in=V((BAND - N, L), BF16),
        agg_grad=V((BAND, L), BF16),
        scat=V((ALL, L), BF16),
        band_grad=V((BAND, L), F32),
        node_out=V((BAND, L), BF16),
        node_in=V((BAND - N, L), BF16),
        n_out=V((n_rows, LANES), BF16),
        n_land=V((n_rows, LANES), BF16),
        n_z_lo=V((Z_LO, n_rows // G, LANES), BF16),
        n_z_hi=V((Z_HI, n_rows // G, LANES), BF16),
        e_out=V((e_rows, LANES), BF16),
        e_land=V((e_rows, LANES), BF16),
        e_z_lo=V((Z_LO, e_rows // G, LANES), BF16),
        e_z_hi=V((Z_HI, e_rows // G, LANES), BF16),
        bias0=V((H, 8, LANES), F32),
        bias1=V((Y_HI * CORES, 8, LANES), F32),
        bias2=V((Z_LO, 8, LANES), F32),
        bias3=V((Z_HI, 8, LANES), F32),
    )
    DMA = pltpu.SemaphoreType.DMA
    scratch.update(load_sem=DMA((3,)), s_sem=DMA((8,)), r_sem=DMA((8,)), n_s=DMA((4,)), n_r=DMA((4,)))
    scratch.update(e_s=DMA((4,)), e_r=DMA((4,)), bias_s=DMA((4,)), bias_r=DMA((4,)))
    node, edge, node_sums, edge_sums, bias = pl.pallas_call(
        functools.partial(kernel, dims, list(inputs) + list(outputs) + list(scratch)),
        out_shape=[jax.ShapeDtypeStruct(shape, dtype) for shape, dtype, _ in outputs.values()],
        in_specs=[pl.BlockSpec(memory_space=space) for _, space in inputs.values()],
        out_specs=[pl.BlockSpec(memory_space=space) for _, _, space in outputs.values()],
        scratch_shapes=list(scratch.values()),
        compiler_params=pltpu.CompilerParams(
            collective_id=0, has_side_effects=True, vmem_limit_bytes=VMEM_BYTES
        ),
        name="layer_back",
    )(*[x for x, _ in inputs.values()])
    shapes = [(N, L), (E, L), (3 * L, L), (1, L), (L, L), (1, L), (2 * L, L), (1, L), (L, L), (1, L)]
    out = pl.pallas_call(
        functools.partial(finish, dims),
        out_shape=[jax.ShapeDtypeStruct(shape, BF16 if i == 1 else F32) for i, shape in enumerate(shapes)],
        in_specs=[pl.BlockSpec(memory_space=ANY)] * 5,
        out_specs=[pl.BlockSpec(memory_space=V)] * 10,
        scratch_shapes=[V((n_rows, LANES), BF16), V((e_rows, LANES), BF16), V((8, LANES), F32), DMA((5,))],
        compiler_params=pltpu.CompilerParams(vmem_limit_bytes=VMEM_BYTES),
        name="finish",
    )(node, edge, node_sums, edge_sums, bias)
    return tuple(x.reshape(L) if x.shape[0] == 1 else x for x in out)


def solution(mesh):
    rows = P(("band", "helper"), None)
    flat = P(("band", "helper"))
    in_specs = (rows,) * 4 + (flat, flat, P(), P("band", None), flat) + (P(),) * 8
    out_specs = (rows, rows) + (P(),) * 8
    return jax.shard_map(on_device, mesh=mesh, in_specs=in_specs, out_specs=out_specs, check_vma=False)
```

```python
import functools
import math
from types import SimpleNamespace

import jax
import jax.numpy as jnp
from jax import lax
from jax.experimental import pallas as pl
from jax.experimental.pallas import tpu as pltpu
from jax.sharding import PartitionSpec as P

Y_HI = 2
Y_LO = 2
Z_HI = 4
Z_LO = 4
CORES = 2
EB = 128
EARLY = 3
ROWS = 256
LANES = 128
VMEM_BYTES = 56 * 1024 * 1024

norm_eps = 1e-05
F32 = jnp.float32
BF16 = jnp.bfloat16
MESH = pl.DeviceIdType.MESH


def dot(a, b):
    return jnp.dot(a, b, preferred_element_type=F32)


def dot_nt(a, b):
    return lax.dot_general(a, b, (((1,), (1,)), ((), ())), preferred_element_type=F32)


def layer_norm(pre_act):
    row_mean = jnp.mean(pre_act, axis=-1, keepdims=True)
    centre = pre_act - row_mean
    inv_dev = lax.rsqrt(jnp.mean(centre * centre, axis=-1, keepdims=True) + norm_eps)
    return centre * inv_dev, inv_dev


def norm_back(grad_in, normed, inv_dev):
    return inv_dev * (
        grad_in
        - jnp.mean(grad_in, axis=-1, keepdims=True)
        - normed * jnp.mean(grad_in * normed, axis=-1, keepdims=True)
    )


def column(row):
    n = row.shape[1]
    diag = lax.broadcasted_iota(jnp.int32, (n, n), 0) == lax.broadcasted_iota(jnp.int32, (n, n), 1)
    return jnp.sum(jnp.where(diag, row, 0.0), axis=1, keepdims=True)


def onehot_cols(col, width):
    ids = lax.broadcasted_iota(jnp.int32, (col.shape[0], width), 1).astype(F32)
    return jnp.where(ids == col, 1.0, 0.0).astype(BF16)


def onehot_rows(row, height):
    ids = lax.broadcasted_iota(jnp.int32, (height, row.shape[1]), 0).astype(F32)
    return jnp.where(ids == row, 1.0, 0.0).astype(BF16)


def at(index, size):
    return pl.ds(pl.multiple_of(index * size, size), size)


def loop(count, body):
    if count == 1:
        body(0)
        return

    def step(i, carry):
        body(i)
        return carry

    lax.fori_loop(0, count, step, 0)


class Flow:
    def __init__(self, flows, send_sem, recv_sem, sent, landed):
        self.send_sem, self.recv_sem, self.sent, self.landed = send_sem, recv_sem, sent, landed
        self.arrived = False
        flows.append(self)

    def send(self, src, dst, device):
        pltpu.make_async_remote_copy(
            src_ref=src,
            dst_ref=dst,
            send_sem=self.send_sem,
            recv_sem=self.recv_sem,
            device_id=device,
            device_id_type=MESH,
        ).start()

    def wait(self):
        self.arrived = True
        pltpu.make_async_copy(self.landed, self.landed, self.recv_sem).wait()

    def drain(self):
        if not self.arrived:
            self.wait()
        pltpu.make_async_copy(self.sent, self.sent, self.send_sem).wait()


class Local:
    def __init__(self, flows, src, dst, sem):
        self.copy = pltpu.make_async_copy(src, dst, sem)
        self.copy.start()
        self.arrived = False
        flows.append(self)

    def wait(self):
        self.arrived = True
        self.copy.wait()

    def drain(self):
        if not self.arrived:
            self.wait()


def kernel(dims, names, *refs):
    flows = []
    r = SimpleNamespace(**dict(zip(names, refs)))
    r.n = SimpleNamespace(out=r.n_out, land=r.n_land, z_lo=r.n_z_lo, z_hi=r.n_z_hi, full=r.n_full, s=r.n_s, r=r.n_r)
    r.e = SimpleNamespace(out=r.e_out, land=r.e_land, z_lo=r.e_z_lo, z_hi=r.e_z_hi, full=r.e_full, s=r.e_s, r=r.e_r)
    steps(dims, r, flows)
    for flow in flows:
        flow.drain()


def steps(dims, r, flows):
    H, E, N, HALO, L, G = dims.H, dims.E, dims.N, dims.HALO, dims.L, dims.G
    BAND = N * H
    LOOK = BAND + 2 * HALO
    ALL = LOOK + BAND
    NBLK = E // ROWS
    ZN = Z_HI * Z_LO

    band = lax.axis_index("band")
    helper = lax.axis_index("helper")
    n_band = Y_HI * ZN * CORES
    core = lax.rem(band, CORES)
    z = lax.rem(lax.div(band, CORES), ZN)
    y_hi = lax.div(band, CORES * ZN)
    z_lo = lax.rem(z, Z_LO)
    z_hi = lax.div(z, Z_LO)
    plane = y_hi * CORES + core
    me = plane * H + helper
    X = H // Y_LO
    x, y = lax.rem(helper, X), y_hi * Y_LO + lax.div(helper, X)
    KINDS = 4
    kind_own = lax.rem(x + y + 2 * core, KINDS)

    def owner(kind, j):
        to_y, to_core = lax.rem(y + j // CORES, Y_HI * Y_LO), lax.rem(core + j % CORES, CORES)
        to_x = lax.rem(kind + 2 * KINDS - to_y - 2 * to_core, KINDS)
        to_plane = lax.div(to_y, Y_LO) * CORES + to_core
        to_helper = lax.rem(to_y, Y_LO) * X + to_x
        return to_plane * H + to_helper, (to_core * KINDS + kind) * (Y_HI * Y_LO) + to_y, place(to_plane, z, to_helper)

    def place(plane_i, z_i, helper_i):
        return dict(
            band=(lax.div(plane_i, CORES) * ZN + z_i) * CORES + lax.rem(plane_i, CORES),
            helper=helper_i,
        )

    def in_group(k):
        g = lax.rem(me + k, G)
        return g, place(lax.div(g, H), z, lax.rem(g, H))

    def in_core(k):
        t = lax.rem(y_hi * H + helper + k, Y_HI * H)
        return place(lax.div(t, H) * CORES + core, z, lax.rem(t, H))

    def in_helper(k):
        return dict(band=band, helper=lax.rem(helper + k, H))

    def in_plane(k):
        return place(lax.rem(plane + k, Y_HI * CORES), z, helper)

    def in_z_lo(k):
        return place(plane, z_hi * Z_LO + lax.rem(z_lo + k, Z_LO), helper)

    def in_z_hi(k):
        return place(plane, lax.rem(z_hi + k, Z_HI) * Z_LO + z_lo, helper)

    next_band = dict(band=lax.rem(band + 1, n_band), helper=helper)
    prev_band = dict(band=lax.rem(band + n_band - 1, n_band), helper=helper)

    def flow(i, sent, landed):
        return Flow(flows, r.s_sem.at[i], r.r_sem.at[i], sent, landed)

    load_edge = Local(flows, r.edge_hbm, r.edge, r.load_sem.at[0])
    load_grad = Local(flows, r.gedge_hbm, r.gedge, r.load_sem.at[1])

    barrier = pltpu.get_barrier_semaphore()

    def greet(device):
        pl.semaphore_signal(barrier, inc=1, device_id=device, device_id_type=MESH)

    for k in range(1, G):
        greet(in_group(k)[1])
    for k in range(1, Z_LO):
        greet(in_z_lo(k))
    for k in range(1, Z_HI):
        greet(in_z_hi(k))
    greet(next_band)
    greet(prev_band)
    hot, hot_t = r.hot, r.hot_t

    def block_onehots(j):
        rows = at(j, EB)
        s_row, r_row = r.send_ids[pl.ds(j, 1), :].astype(F32), r.recv_ids[pl.ds(j, 1), :].astype(F32)
        hot[rows, :LOOK] = onehot_cols(column(s_row), LOOK)
        hot[rows, LOOK:] = onehot_cols(column(r_row), BAND)
        hot_t[:LOOK, rows] = onehot_rows(s_row, LOOK)
        hot_t[LOOK:, rows] = onehot_rows(r_row, BAND)

    loop(EARLY, block_onehots)
    pl.semaphore_wait(barrier, G - 1 + Z_LO - 1 + Z_HI - 1 + 2)

    look, proj = r.look, r.proj
    others = look.at[pl.ds(0, (H - 1) * N)]
    rows_flow = flow(0, others, others)
    for k in range(1, H):
        rows_flow.send(r.node, look.at[at(helper, N)], in_helper(k))
    look[at(helper, N), :] = r.node[...]


    loop(E // EB - EARLY, lambda j: block_onehots(j + EARLY))
    halo_row = r.halo[...].astype(F32)
    halo_t = onehot_rows(halo_row, BAND)
    r.halo_t[:, :HALO] = halo_t
    r.halo_t[:, HALO:] = halo_t
    sea = column(r.sea[...].astype(F32))

    live_blocks = r.band_edges[band]
    slot = lax.shift_right_logical(lax.broadcasted_iota(jnp.int32, (E, 1), 0), int(math.log2(EB)))
    r.live[...] = jnp.where(slot * H + helper < live_blocks, 1.0, 0.0)

    load_edge.wait()
    edge, pre = r.edge, r.pre

    def edge_part(i):
        rows = at(i, ROWS)
        block = edge[rows, :]
        pre[rows, :] = dot(block, r.ew1[2 * L :, :]) + r.eb1[...]
        r.edge_t[:, rows] = block.T

    loop(NBLK, edge_part)

    rows_flow.wait()
    r.halo_out[...] = dot(onehot_cols(column(halo_row), BAND), look[:BAND, :]).astype(BF16)
    from_prev, from_next = look.at[pl.ds(BAND, HALO)], look.at[pl.ds(BAND + HALO, HALO)]
    halo_up = flow(1, r.halo_out, from_prev)
    halo_down = flow(2, r.halo_out, from_next)
    halo_up.send(r.halo_out, from_prev, next_band)
    halo_down.send(r.halo_out, from_next, prev_band)

    def project(i):
        rows = at(i, EB)
        block = look[rows, :]
        proj[rows, :] = dot(block, r.ew1[:L, :]).astype(BF16)
        proj[pl.ds(pl.multiple_of(LOOK + i * EB, EB), EB), :] = dot(block, r.ew1[L : 2 * L, :]).astype(BF16)

    loop(BAND // EB, project)

    def own_part(i):
        rows = at(i, ROWS)
        pre[rows, :] += dot(hot[rows, :BAND], proj[:BAND, :]) + dot(hot[rows, LOOK:], proj[LOOK:, :])

    loop(NBLK, own_part)
    halo_up.wait()
    halo_down.wait()
    proj[BAND:LOOK, :] = dot(look[BAND:, :], r.ew1[:L, :]).astype(BF16)

    hidden, normed, inv, msg = r.hidden, r.normed, r.inv, r.msg

    def edge_forward(i):
        rows = at(i, ROWS)
        pre_act = pre[rows, :] + dot(hot[rows, BAND:LOOK], proj[BAND:LOOK, :])
        sig = jax.nn.sigmoid(pre_act)
        hid = (pre_act * sig).astype(BF16)
        hidden[rows, :] = hid
        pre[rows, :] = sig * (1.0 + pre_act * (1.0 - sig))
        norm, inv_dev = layer_norm(dot(hid, r.ew2[...]) + r.eb2[...])
        normed[rows, :] = norm
        inv[rows, :] = inv_dev
        msg[rows, :] = (norm * r.live[rows, :]).astype(BF16)

    loop(NBLK, edge_forward)

    agg_out, agg_in = r.agg_out, r.agg_in

    def sum_messages(i):
        agg_out[at(i, EB), :] = dot(hot_t[pl.ds(pl.multiple_of(LOOK + i * EB, EB), EB), :], msg[...]).astype(BF16)

    loop(BAND // EB, sum_messages)
    agg_flow = flow(3, others, agg_in)
    for k in range(1, H):
        to = in_helper(k)
        agg_flow.send(agg_out.at[at(lax.rem(helper + k, H), N)], agg_in.at[pl.ds((k - 1) * N, N)], to)

    def hidden_turn(i):
        rows = at(i, ROWS)
        r.hidden_t[:, rows] = hidden[rows, :].T

    def look_turn(i):
        rows = at(i, EB)
        r.look_t[:, rows] = look[rows, :].T

    loop(NBLK, hidden_turn)
    loop(LOOK // EB, look_turn)
    agg_flow.wait()
    agg = agg_out[at(helper, N), :].astype(F32)
    for k in range(H - 1):
        agg += agg_in[k * N : (k + 1) * N, :].astype(F32)
    agg = agg.astype(BF16)

    node = r.node[...]
    nw1 = r.nw1
    n_pre = dot(node, nw1[:L, :]) + dot(agg, nw1[L:, :]) + r.nb1[...]
    n_sig = jax.nn.sigmoid(n_pre)
    n_hid = (n_pre * n_sig).astype(BF16)
    n_norm, n_inv = layer_norm(dot(n_hid, r.nw2[...]) + r.nb2[...])
    g_node = r.gnode[...].astype(F32)
    n_dz = norm_back(sea * g_node, n_norm, n_inv)
    n_dz_b = n_dz.astype(BF16)
    n_dpre = dot_nt(n_dz_b, r.nw2[...]) * (n_sig * (1.0 + n_pre * (1.0 - n_sig)))
    n_dpre_b = n_dpre.astype(BF16)
    agg_grad = r.agg_grad
    mine = agg_grad.at[at(helper, N)]
    agg_grad[at(helper, N), :] = dot_nt(n_dpre_b, nw1[L:, :]).astype(BF16)
    back_flow = flow(4, others, agg_grad.at[pl.ds(0, (H - 1) * N)])
    for k in range(1, H):
        back_flow.send(mine, mine, in_helper(k))

    own = (core * KINDS + kind_own) * (Y_HI * Y_LO) + y
    node_sums = Reduced(flows, r.n, dims, me, me, z_lo, z_hi, in_group, in_core, in_z_lo, in_z_hi)
    edge_sums = Reduced(flows, r.e, dims, me, own, z_lo, z_hi, in_group, in_core, in_z_lo, in_z_hi)

    bias_axes = (
        (r.bias0, H, helper, in_helper),
        (r.bias1, Y_HI * CORES, plane, in_plane),
        (r.bias2, Z_LO, z_lo, in_z_lo),
        (r.bias3, Z_HI, z_hi, in_z_hi),
    )

    def bias_send(step):
        ref, count, slot_i, device_of = bias_axes[step]
        mine = ref.at[slot_i]
        rest = ref.at[pl.ds(0, count - 1)]
        bias_flow = Flow(flows, r.bias_s.at[step], r.bias_r.at[step], rest, rest)
        for k in range(1, count):
            bias_flow.send(mine, mine, device_of(k))
        return bias_flow

    def bias_sum(step, bias_flow):
        ref, count = bias_axes[step][:2]
        bias_flow.wait()
        total = ref[0]
        for k in range(1, count):
            total += ref[k]
        return total

    node_sums.put(0, dot(node.T, n_dpre_b))
    node_sums.put(L, dot(agg.T, n_dpre_b))
    node_sums.put(2 * L, dot(n_hid.T, n_dz_b))
    node_sums.scatter()
    node_din = g_node + dot_nt(n_dpre_b, nw1[:L, :])

    load_grad.wait()
    gedge, dz_b, dpre_b = r.gedge, r.dz_b, r.dpre_b
    back_flow.wait()

    def edge_back(i, sums):
        rows = at(i, ROWS)
        grad = gedge[rows, :].astype(F32) + dot(hot[rows, LOOK:], agg_grad[...])
        dz = norm_back(grad * r.live[rows, :], normed[rows, :], inv[rows, :])
        second = dz.astype(BF16)
        dz_b[rows, :] = second
        dpre = dot_nt(second, r.ew2[...]) * pre[rows, :]
        dpre_b[rows, :] = dpre.astype(BF16)
        return sums[0] + jnp.sum(dpre, axis=0, keepdims=True), sums[1] + jnp.sum(dz, axis=0, keepdims=True)

    zero = jnp.zeros((1, L), F32)
    e_gb1, e_gb2 = lax.fori_loop(0, NBLK, edge_back, (zero, zero))

    scat = r.scat

    def scatter(i):
        rows = at(i, ROWS)
        scat[rows, :] = dot(hot_t[rows, :], dpre_b[...]).astype(BF16)

    edge_sums.put(3 * L, dot(r.hidden_t[...], dz_b[...]))
    edge_sums.scatter_kind(3, owner)
    edge_sums.put(2 * L, dot(r.edge_t[...], dpre_b[...]))
    edge_sums.scatter_kind(2, owner)
    loop(BAND // ROWS, lambda i: scatter(LOOK // ROWS + i))
    edge_sums.put(L, dot(r.look_t[:, :BAND], scat[LOOK:, :]))
    edge_sums.scatter_kind(1, owner)
    loop(LOOK // ROWS, scatter)
    edge_sums.put(0, dot(r.look_t[...], scat[:LOOK, :]))
    edge_sums.scatter_kind(0, owner)
    node_sums.along_z_lo()

    tiles = (e_gb1, e_gb2, jnp.sum(n_dpre, axis=0, keepdims=True), jnp.sum(n_dz, axis=0, keepdims=True))
    for i, row in enumerate(tiles):
        r.bias0[helper, 2 * i : 2 * i + 1, :] = row[:, :LANES]
        r.bias0[helper, 2 * i + 1 : 2 * i + 2, :] = row[:, LANES:]
    bias_flow = bias_send(0)

    halo_back, halo_in = r.halo_back, r.halo_in
    halo_back[...] = dot_nt(scat[BAND:LOOK, :], r.ew1[:L, :]).astype(BF16)
    upper, lower = pl.ds(0, HALO), pl.ds(HALO, HALO)
    back_down = flow(5, halo_back.at[upper], halo_in.at[upper])
    back_up = flow(6, halo_back.at[lower], halo_in.at[lower])
    back_down.send(halo_back.at[upper], halo_in.at[upper], prev_band)
    back_up.send(halo_back.at[lower], halo_in.at[lower], next_band)

    node_sums.along_z_hi()

    band_grad = r.band_grad
    band_grad[...] = dot_nt(scat[:BAND, :], r.ew1[:L, :]) + dot_nt(scat[LOOK:, :], r.ew1[L : 2 * L, :])

    r.bias1[plane] = bias_sum(0, bias_flow)
    bias_flow = bias_send(1)
    edge_sums.along_z_lo()

    back_down.wait()
    back_up.wait()
    node_out, node_in = r.node_out, r.node_in
    node_out[...] = (band_grad[...] + dot(r.halo_t[...], halo_in[...])).astype(BF16)
    node_flow = flow(7, others, node_in)
    for k in range(1, H):
        to = in_helper(k)
        node_flow.send(node_out.at[at(lax.rem(helper + k, H), N)], node_in.at[pl.ds((k - 1) * N, N)], to)

    r.bias2[z_lo] = bias_sum(1, bias_flow)
    bias_flow = bias_send(2)
    edge_sums.along_z_hi()

    node_sums.gather()

    def edge_grad(i):
        rows = at(i, ROWS)
        din = dot_nt(dpre_b[rows, :], r.ew1[2 * L :, :])
        r.edge_new[rows, :] = ((gedge[rows, :].astype(F32) + din) * r.live[rows, :]).astype(BF16)

    loop(NBLK, edge_grad)
    Local(flows, r.edge_new, r.o_edge, r.load_sem.at[2])

    r.bias3[z_hi] = bias_sum(2, bias_flow)
    bias_flow = bias_send(3)
    edge_sums.gather()

    mate = place(y_hi * CORES + 1 - core, z, helper)
    node_sums.hand_on(mate, [(i * CORES + core) * H for i in range(Y_HI)])
    node_flow.wait()
    total = node_out[at(helper, N), :].astype(F32)
    for k in range(H - 1):
        total += node_in[k * N : (k + 1) * N, :].astype(F32)
    r.o_node[...] = total + node_din
    r.o_bias[...] = bias_sum(3, bias_flow)
    edge_sums.hand_on(mate, [core * (G // CORES)])
    node_sums.handed.wait()
    edge_sums.handed.wait()


class Reduced:
    def __init__(self, flows, refs, dims, me, own, z_lo, z_hi, in_group, in_core, in_z_lo, in_z_hi):
        self.flows, self.refs, self.me, self.own, self.z_lo, self.z_hi = flows, refs, me, own, z_lo, z_hi
        self.in_group, self.in_core, self.in_z_lo, self.in_z_hi = in_group, in_core, in_z_lo, in_z_hi
        self.G = dims.G
        self.piece = refs.out.shape[0] // dims.G
        rest = pl.ds(0, (self.G - 1) * self.piece)
        self.first = self.flow(0, refs.out.at[rest], refs.land.at[rest])

    def flow(self, i, sent, landed):
        return Flow(self.flows, self.refs.s.at[i], self.refs.r.at[i], sent, landed)

    def put(self, first, value):
        out = self.refs.out
        half, count = out.shape[0] // 2, value.shape[0]
        out[first : first + count, :] = value[:, :LANES].astype(BF16)
        out[half + first : half + first + count, :] = value[:, LANES:].astype(BF16)

    def scatter_to(self, g, piece_i, device):
        piece = self.piece
        self.first.send(self.refs.out.at[at(piece_i, piece)], self.refs.land.at[at(self.me, piece)], device)

    def scatter(self):
        for k in range(1, self.G):
            g, to = self.in_group(k)
            self.scatter_to(g, g, to)

    def scatter_kind(self, kind, owner):
        for j in range(self.G // 4):
            g, piece_i, to = owner(kind, j)

            @pl.when(g != self.me)
            def _():
                self.scatter_to(g, piece_i, to)

    def along_z_lo(self):
        out, land, quad, piece = self.refs.out, self.refs.land, self.refs.z_lo, self.piece
        self.first.wait()
        land[at(self.me, piece), :] = out[at(self.own, piece), :]
        zero = jnp.zeros((piece, LANES), F32)
        total = lax.fori_loop(0, self.G, lambda k, acc: acc + land[at(k, piece), :].astype(F32), zero)
        mine = quad.at[self.z_lo]
        quad[self.z_lo] = total.astype(BF16)
        rest = quad.at[pl.ds(0, Z_LO - 1)]
        self.second = self.flow(1, rest, rest)
        for k in range(1, Z_LO):
            self.second.send(mine, mine, self.in_z_lo(k))

    def along_z_hi(self):
        old, quad = self.refs.z_lo, self.refs.z_hi
        self.second.wait()
        total = old[0].astype(F32)
        for k in range(1, Z_LO):
            total += old[k].astype(F32)
        mine = quad.at[self.z_hi]
        quad[self.z_hi] = total.astype(BF16)
        rest = quad.at[pl.ds(0, Z_HI - 1)]
        self.third = self.flow(2, rest, rest)
        for k in range(1, Z_HI):
            self.third.send(mine, mine, self.in_z_hi(k))

    def gather(self):
        quad, full, piece, half = self.refs.z_hi, self.refs.full, self.piece, self.G // 2
        self.third.wait()
        total = quad[0].astype(F32)
        for k in range(1, Z_HI):
            total += quad[k].astype(F32)
        mine = full.at[at(self.own, piece)]
        full[at(self.own, piece), :] = total.astype(BF16)
        rest = full.at[pl.ds(0, (half - 1) * piece)]
        self.done = self.flow(3, rest, rest)
        for k in range(1, half):
            self.done.send(mine, mine, self.in_core(k))

    def hand_on(self, mate, firsts):
        full, half = self.refs.full, self.G // 2
        self.done.wait()
        whole = full.at[pl.ds(0, half * self.piece)]
        self.handed = self.flow(4, whole, whole)
        count = half * self.piece // len(firsts)
        for first in firsts:
            part = full.at[pl.ds(pl.multiple_of(first * self.piece, 16), count)]
            self.handed.send(part, part, mate)


def finish(dims, node_hbm, edge_hbm, node_sums_hbm, edge_sums_hbm, bias_hbm, o_node, o_edge, *rest):
    o_ew1, o_eb1, o_ew2, o_eb2, o_nw1, o_nb1, o_nw2, o_nb2, node_sums, edge_sums, bias, sems = rest
    pairs = (
        (edge_sums_hbm, edge_sums),
        (node_sums_hbm, node_sums),
        (bias_hbm, bias),
        (edge_hbm, o_edge),
        (node_hbm, o_node),
    )
    copies = [pltpu.make_async_copy(src, dst, sems.at[i]) for i, (src, dst) in enumerate(pairs)]
    for copy in copies:
        copy.start()

    def weights(full, targets, scale):
        half, first = full.shape[0] // 2, 0
        for out in targets:
            count = out.shape[0]
            out[:, :LANES] = full[first : first + count, :].astype(F32) * scale
            out[:, LANES:] = full[half + first : half + first + count, :].astype(F32) * scale
            first += count

    copies[0].wait()
    weights(edge_sums, (o_ew1, o_ew2), dims.edge_scale)
    copies[1].wait()
    weights(node_sums, (o_nw1, o_nw2), dims.node_scale)
    copies[2].wait()
    for i, (out, scale) in enumerate(
        ((o_eb1, dims.edge_scale), (o_eb2, dims.edge_scale), (o_nb1, dims.node_scale), (o_nb2, dims.node_scale))
    ):
        out[:, :LANES] = bias[2 * i : 2 * i + 1, :] * scale
        out[:, LANES:] = bias[2 * i + 1 : 2 * i + 2, :] * scale
    copies[3].wait()
    copies[4].wait()


def on_device(
    node_latent,
    edge_latent,
    grad_out_node,
    grad_out_edge,
    senders,
    receivers,
    band_edges,
    halo_list,
    sea_mask,
    edge_w1,
    edge_b1,
    edge_w2,
    edge_b2,
    node_w1,
    node_b1,
    node_w2,
    node_b2,
):
    H = lax.axis_size("helper")
    bands = lax.axis_size("band")
    N, L = node_latent.shape
    E = edge_latent.shape[0]
    HALO = halo_list.shape[1]
    BAND = N * H
    LOOK = BAND + 2 * HALO
    ALL = LOOK + BAND
    G = H * Y_HI * CORES
    dims = SimpleNamespace(
        H=H,
        E=E,
        N=N,
        HALO=HALO,
        L=L,
        G=G,
        edge_scale=1.0 / math.sqrt(E * H * bands),
        node_scale=1.0 / math.sqrt(N * H * bands),
    )
    V, S, ANY = pltpu.VMEM, pltpu.SMEM, pl.ANY
    inputs = dict(
        node=(node_latent, V),
        edge_hbm=(edge_latent, ANY),
        gnode=(grad_out_node, V),
        gedge_hbm=(grad_out_edge, ANY),
        send_ids=(senders.reshape(E // EB, EB), V),
        recv_ids=(receivers.reshape(E // EB, EB), V),
        band_edges=(band_edges, S),
        halo=(halo_list, V),
        sea=(sea_mask.reshape(1, N), V),
        ew1=(edge_w1, V),
        eb1=(edge_b1.reshape(1, L), V),
        ew2=(edge_w2, V),
        eb2=(edge_b2.reshape(1, L), V),
        nw1=(node_w1, V),
        nb1=(node_b1.reshape(1, L), V),
        nw2=(node_w2, V),
        nb2=(node_b2.reshape(1, L), V),
    )
    n_rows, e_rows = 3 * L * (L // LANES), 4 * L * (L // LANES)
    outputs = dict(
        o_node=((N, L), F32, V),
        o_edge=((E, L), BF16, ANY),
        n_full=((n_rows, LANES), BF16, V),
        e_full=((e_rows, LANES), BF16, V),
        o_bias=((8, LANES), F32, V),
    )
    scratch = dict(
        edge=V((E, L), BF16),
        gedge=V((E, L), BF16),
        edge_new=V((E, L), BF16),
        look=V((LOOK, L), BF16),
        look_t=V((L, LOOK), BF16),
        edge_t=V((L, E), BF16),
        hidden_t=V((L, E), BF16),
        proj=V((ALL, L), BF16),
        hot=V((E, ALL), BF16),
        hot_t=V((ALL, E), BF16),
        halo_t=V((BAND, 2 * HALO), BF16),
        halo_out=V((HALO, L), BF16),
        halo_back=V((2 * HALO, L), BF16),
        halo_in=V((2 * HALO, L), BF16),
        live=V((E, 1), F32),
        pre=V((E, L), F32),
        hidden=V((E, L), BF16),
        normed=V((E, L), F32),
        inv=V((E, 1), F32),
        msg=V((E, L), BF16),
        dz_b=V((E, L), BF16),
        dpre_b=V((E, L), BF16),
        agg_out=V((BAND, L), BF16),
        agg_in=V((BAND - N, L), BF16),
        agg_grad=V((BAND, L), BF16),
        scat=V((ALL, L), BF16),
        band_grad=V((BAND, L), F32),
        node_out=V((BAND, L), BF16),
        node_in=V((BAND - N, L), BF16),
        n_out=V((n_rows, LANES), BF16),
        n_land=V((n_rows, LANES), BF16),
        n_z_lo=V((Z_LO, n_rows // G, LANES), BF16),
        n_z_hi=V((Z_HI, n_rows // G, LANES), BF16),
        e_out=V((e_rows, LANES), BF16),
        e_land=V((e_rows, LANES), BF16),
        e_z_lo=V((Z_LO, e_rows // G, LANES), BF16),
        e_z_hi=V((Z_HI, e_rows // G, LANES), BF16),
        bias0=V((H, 8, LANES), F32),
        bias1=V((Y_HI * CORES, 8, LANES), F32),
        bias2=V((Z_LO, 8, LANES), F32),
        bias3=V((Z_HI, 8, LANES), F32),
    )
    DMA = pltpu.SemaphoreType.DMA
    scratch.update(load_sem=DMA((3,)), s_sem=DMA((8,)), r_sem=DMA((8,)), n_s=DMA((5,)), n_r=DMA((5,)))
    scratch.update(e_s=DMA((5,)), e_r=DMA((5,)), bias_s=DMA((4,)), bias_r=DMA((4,)))
    node, edge, node_sums, edge_sums, bias = pl.pallas_call(
        functools.partial(kernel, dims, list(inputs) + list(outputs) + list(scratch)),
        out_shape=[jax.ShapeDtypeStruct(shape, dtype) for shape, dtype, _ in outputs.values()],
        in_specs=[pl.BlockSpec(memory_space=space) for _, space in inputs.values()],
        out_specs=[pl.BlockSpec(memory_space=space) for _, _, space in outputs.values()],
        scratch_shapes=list(scratch.values()),
        compiler_params=pltpu.CompilerParams(
            collective_id=0, has_side_effects=True, vmem_limit_bytes=VMEM_BYTES
        ),
        name="layer_back",
    )(*[x for x, _ in inputs.values()])
    shapes = [(N, L), (E, L), (3 * L, L), (1, L), (L, L), (1, L), (2 * L, L), (1, L), (L, L), (1, L)]
    out = pl.pallas_call(
        functools.partial(finish, dims),
        out_shape=[jax.ShapeDtypeStruct(shape, BF16 if i == 1 else F32) for i, shape in enumerate(shapes)],
        in_specs=[pl.BlockSpec(memory_space=ANY)] * 5,
        out_specs=[pl.BlockSpec(memory_space=V)] * 10,
        scratch_shapes=[V((n_rows, LANES), BF16), V((e_rows, LANES), BF16), V((8, LANES), F32), DMA((5,))],
        compiler_params=pltpu.CompilerParams(vmem_limit_bytes=VMEM_BYTES),
        name="finish",
    )(node, edge, node_sums, edge_sums, bias)
    return tuple(x.reshape(L) if x.shape[0] == 1 else x for x in out)


def solution(mesh):
    rows = P(("band", "helper"), None)
    flat = P(("band", "helper"))
    in_specs = (rows,) * 4 + (flat, flat, P(), P("band", None), flat) + (P(),) * 8
    out_specs = (rows, rows) + (P(),) * 8
    return jax.shard_map(on_device, mesh=mesh, in_specs=in_specs, out_specs=out_specs, check_vma=False)
```

```python
import functools
import math
from types import SimpleNamespace

import jax
import jax.numpy as jnp
from jax import lax
from jax.experimental import pallas as pl
from jax.experimental.pallas import tpu as pltpu
from jax.sharding import PartitionSpec as P

Y_HI = 2
Y_LO = 2
Z_HI = 4
Z_LO = 4
CORES = 2
EB = 128
EARLY = 3
ROWS = 256
LANES = 128
VMEM_BYTES = 56 * 1024 * 1024

norm_eps = 1e-05
F32 = jnp.float32
BF16 = jnp.bfloat16
MESH = pl.DeviceIdType.MESH


def dot(a, b):
    return jnp.dot(a, b, preferred_element_type=F32)


def dot_nt(a, b):
    return lax.dot_general(a, b, (((1,), (1,)), ((), ())), preferred_element_type=F32)


def layer_norm(pre_act):
    row_mean = jnp.mean(pre_act, axis=-1, keepdims=True)
    centre = pre_act - row_mean
    inv_dev = lax.rsqrt(jnp.mean(centre * centre, axis=-1, keepdims=True) + norm_eps)
    return centre * inv_dev, inv_dev


def norm_back(grad_in, normed, inv_dev):
    return inv_dev * (
        grad_in
        - jnp.mean(grad_in, axis=-1, keepdims=True)
        - normed * jnp.mean(grad_in * normed, axis=-1, keepdims=True)
    )


def column(row):
    n = row.shape[1]
    diag = lax.broadcasted_iota(jnp.int32, (n, n), 0) == lax.broadcasted_iota(jnp.int32, (n, n), 1)
    return jnp.sum(jnp.where(diag, row, 0.0), axis=1, keepdims=True)


def onehot_cols(col, width):
    ids = lax.broadcasted_iota(jnp.int32, (col.shape[0], width), 1).astype(F32)
    return jnp.where(ids == col, 1.0, 0.0).astype(BF16)


def onehot_rows(row, height):
    ids = lax.broadcasted_iota(jnp.int32, (height, row.shape[1]), 0).astype(F32)
    return jnp.where(ids == row, 1.0, 0.0).astype(BF16)


def at(index, size):
    return pl.ds(pl.multiple_of(index * size, size), size)


def loop(count, body):
    if count == 1:
        body(0)
        return

    def step(i, carry):
        body(i)
        return carry

    lax.fori_loop(0, count, step, 0)


class Flow:
    def __init__(self, flows, send_sem, recv_sem, sent, landed):
        self.send_sem, self.recv_sem, self.sent, self.landed = send_sem, recv_sem, sent, landed
        self.arrived = False
        flows.append(self)

    def send(self, src, dst, device):
        pltpu.make_async_remote_copy(
            src_ref=src,
            dst_ref=dst,
            send_sem=self.send_sem,
            recv_sem=self.recv_sem,
            device_id=device,
            device_id_type=MESH,
        ).start()

    def wait(self):
        self.arrived = True
        pltpu.make_async_copy(self.landed, self.landed, self.recv_sem).wait()

    def drain(self):
        if not self.arrived:
            self.wait()
        pltpu.make_async_copy(self.sent, self.sent, self.send_sem).wait()


class Local:
    def __init__(self, flows, src, dst, sem):
        self.copy = pltpu.make_async_copy(src, dst, sem)
        self.copy.start()
        self.arrived = False
        flows.append(self)

    def wait(self):
        self.arrived = True
        self.copy.wait()

    def drain(self):
        if not self.arrived:
            self.wait()


def kernel(dims, names, *refs):
    flows = []
    r = SimpleNamespace(**dict(zip(names, refs)))
    r.n = SimpleNamespace(out=r.n_out, land=r.n_land, z_lo=r.n_z_lo, z_hi=r.n_z_hi, full=r.n_full, s=r.n_s, r=r.n_r)
    r.e = SimpleNamespace(out=r.e_out, land=r.e_land, z_lo=r.e_z_lo, z_hi=r.e_z_hi, full=r.e_full, s=r.e_s, r=r.e_r)
    steps(dims, r, flows)
    for flow in flows:
        flow.drain()


def steps(dims, r, flows):
    H, E, N, HALO, L, G = dims.H, dims.E, dims.N, dims.HALO, dims.L, dims.G
    BAND = N * H
    LOOK = BAND + 2 * HALO
    ALL = LOOK + BAND
    NBLK = E // ROWS
    ZN = Z_HI * Z_LO

    band = lax.axis_index("band")
    helper = lax.axis_index("helper")
    n_band = Y_HI * ZN * CORES
    core = lax.rem(band, CORES)
    z = lax.rem(lax.div(band, CORES), ZN)
    y_hi = lax.div(band, CORES * ZN)
    z_lo = lax.rem(z, Z_LO)
    z_hi = lax.div(z, Z_LO)
    plane = y_hi * CORES + core
    me = plane * H + helper
    X = H // Y_LO
    x, y = lax.rem(helper, X), y_hi * Y_LO + lax.div(helper, X)
    KINDS = 4
    kind_own = lax.rem(x + y + 2 * core, KINDS)

    def owner(kind, j):
        to_y, to_core = lax.rem(y + j // CORES, Y_HI * Y_LO), lax.rem(core + j % CORES, CORES)
        to_x = lax.rem(kind + 2 * KINDS - to_y - 2 * to_core, KINDS)
        to_plane = lax.div(to_y, Y_LO) * CORES + to_core
        to_helper = lax.rem(to_y, Y_LO) * X + to_x
        return to_plane * H + to_helper, (to_core * KINDS + kind) * (Y_HI * Y_LO) + to_y, place(to_plane, z, to_helper)

    def place(plane_i, z_i, helper_i):
        return dict(
            band=(lax.div(plane_i, CORES) * ZN + z_i) * CORES + lax.rem(plane_i, CORES),
            helper=helper_i,
        )

    def in_group(k):
        g = lax.rem(me + k, G)
        return g, place(lax.div(g, H), z, lax.rem(g, H))

    def in_core(k):
        t = lax.rem(y_hi * H + helper + k, Y_HI * H)
        return place(lax.div(t, H) * CORES + core, z, lax.rem(t, H))

    def in_helper(k):
        return dict(band=band, helper=lax.rem(helper + k, H))

    def in_plane(k):
        return place(lax.rem(plane + k, Y_HI * CORES), z, helper)

    def in_z_lo(k):
        return place(plane, z_hi * Z_LO + lax.rem(z_lo + k, Z_LO), helper)

    def in_z_hi(k):
        return place(plane, lax.rem(z_hi + k, Z_HI) * Z_LO + z_lo, helper)

    next_band = dict(band=lax.rem(band + 1, n_band), helper=helper)
    prev_band = dict(band=lax.rem(band + n_band - 1, n_band), helper=helper)

    def flow(i, sent, landed):
        return Flow(flows, r.s_sem.at[i], r.r_sem.at[i], sent, landed)

    load_edge = Local(flows, r.edge_hbm, r.edge, r.load_sem.at[0])
    load_ew1 = Local(flows, r.ew1_hbm, r.ew1, r.load_sem.at[3])
    load_ew2 = Local(flows, r.ew2_hbm, r.ew2, r.load_sem.at[4])
    load_nw1 = Local(flows, r.nw1_hbm, r.nw1, r.load_sem.at[5])
    load_nw2 = Local(flows, r.nw2_hbm, r.nw2, r.load_sem.at[6])
    load_grad = Local(flows, r.gedge_hbm, r.gedge, r.load_sem.at[1])

    barrier = pltpu.get_barrier_semaphore()

    def greet(device):
        pl.semaphore_signal(barrier, inc=1, device_id=device, device_id_type=MESH)

    for k in range(1, G):
        greet(in_group(k)[1])
    for k in range(1, Z_LO):
        greet(in_z_lo(k))
    for k in range(1, Z_HI):
        greet(in_z_hi(k))
    greet(next_band)
    greet(prev_band)
    hot, hot_t = r.hot, r.hot_t

    def block_onehots(j):
        rows = at(j, EB)
        s_row, r_row = r.send_ids[pl.ds(j, 1), :].astype(F32), r.recv_ids[pl.ds(j, 1), :].astype(F32)
        hot[rows, :LOOK] = onehot_cols(column(s_row), LOOK)
        hot[rows, LOOK:] = onehot_cols(column(r_row), BAND)
        hot_t[:LOOK, rows] = onehot_rows(s_row, LOOK)
        hot_t[LOOK:, rows] = onehot_rows(r_row, BAND)

    loop(EARLY, block_onehots)
    pl.semaphore_wait(barrier, G - 1 + Z_LO - 1 + Z_HI - 1 + 2)

    look, proj = r.look, r.proj
    others = look.at[pl.ds(0, (H - 1) * N)]
    rows_flow = flow(0, others, others)
    for k in range(1, H):
        rows_flow.send(r.node, look.at[at(helper, N)], in_helper(k))
    look[at(helper, N), :] = r.node[...]


    loop(E // EB - EARLY, lambda j: block_onehots(j + EARLY))
    halo_row = r.halo[...].astype(F32)
    halo_t = onehot_rows(halo_row, BAND)
    r.halo_t[:, :HALO] = halo_t
    r.halo_t[:, HALO:] = halo_t
    sea = column(r.sea[...].astype(F32))

    live_blocks = r.band_edges[band]
    slot = lax.shift_right_logical(lax.broadcasted_iota(jnp.int32, (E, 1), 0), int(math.log2(EB)))
    r.live[...] = jnp.where(slot * H + helper < live_blocks, 1.0, 0.0)

    load_edge.wait()
    load_ew1.wait()
    load_ew2.wait()
    load_nw1.wait()
    load_nw2.wait()
    edge, pre = r.edge, r.pre

    def edge_part(i):
        rows = at(i, ROWS)
        block = edge[rows, :]
        pre[rows, :] = dot(block, r.ew1[2 * L :, :]) + r.eb1[...]
        r.edge_t[:, rows] = block.T

    loop(NBLK, edge_part)

    rows_flow.wait()
    r.halo_out[...] = dot(onehot_cols(column(halo_row), BAND), look[:BAND, :]).astype(BF16)
    from_prev, from_next = look.at[pl.ds(BAND, HALO)], look.at[pl.ds(BAND + HALO, HALO)]
    halo_up = flow(1, r.halo_out, from_prev)
    halo_down = flow(2, r.halo_out, from_next)
    halo_up.send(r.halo_out, from_prev, next_band)
    halo_down.send(r.halo_out, from_next, prev_band)

    def project(i):
        rows = at(i, EB)
        block = look[rows, :]
        proj[rows, :] = dot(block, r.ew1[:L, :]).astype(BF16)
        proj[pl.ds(pl.multiple_of(LOOK + i * EB, EB), EB), :] = dot(block, r.ew1[L : 2 * L, :]).astype(BF16)

    loop(BAND // EB, project)

    def own_part(i):
        rows = at(i, ROWS)
        pre[rows, :] += dot(hot[rows, :BAND], proj[:BAND, :]) + dot(hot[rows, LOOK:], proj[LOOK:, :])

    loop(NBLK, own_part)
    halo_up.wait()
    halo_down.wait()
    proj[BAND:LOOK, :] = dot(look[BAND:, :], r.ew1[:L, :]).astype(BF16)

    hidden, normed, inv, msg = r.hidden, r.normed, r.inv, r.msg

    def edge_forward(i):
        rows = at(i, ROWS)
        pre_act = pre[rows, :] + dot(hot[rows, BAND:LOOK], proj[BAND:LOOK, :])
        sig = jax.nn.sigmoid(pre_act)
        hid = (pre_act * sig).astype(BF16)
        hidden[rows, :] = hid
        pre[rows, :] = sig * (1.0 + pre_act * (1.0 - sig))
        norm, inv_dev = layer_norm(dot(hid, r.ew2[...]) + r.eb2[...])
        normed[rows, :] = norm
        inv[rows, :] = inv_dev
        msg[rows, :] = (norm * r.live[rows, :]).astype(BF16)

    loop(NBLK, edge_forward)

    agg_out, agg_in = r.agg_out, r.agg_in

    def sum_messages(i):
        agg_out[at(i, EB), :] = dot(hot_t[pl.ds(pl.multiple_of(LOOK + i * EB, EB), EB), :], msg[...]).astype(BF16)

    loop(BAND // EB, sum_messages)
    agg_flow = flow(3, others, agg_in)
    for k in range(1, H):
        to = in_helper(k)
        agg_flow.send(agg_out.at[at(lax.rem(helper + k, H), N)], agg_in.at[pl.ds((k - 1) * N, N)], to)

    def hidden_turn(i):
        rows = at(i, ROWS)
        r.hidden_t[:, rows] = hidden[rows, :].T

    def look_turn(i):
        rows = at(i, EB)
        r.look_t[:, rows] = look[rows, :].T

    loop(NBLK, hidden_turn)
    loop(LOOK // EB, look_turn)
    agg_flow.wait()
    agg = agg_out[at(helper, N), :].astype(F32)
    for k in range(H - 1):
        agg += agg_in[k * N : (k + 1) * N, :].astype(F32)
    agg = agg.astype(BF16)

    node = r.node[...]
    nw1 = r.nw1
    n_pre = dot(node, nw1[:L, :]) + dot(agg, nw1[L:, :]) + r.nb1[...]
    n_sig = jax.nn.sigmoid(n_pre)
    n_hid = (n_pre * n_sig).astype(BF16)
    n_norm, n_inv = layer_norm(dot(n_hid, r.nw2[...]) + r.nb2[...])
    g_node = r.gnode[...].astype(F32)
    n_dz = norm_back(sea * g_node, n_norm, n_inv)
    n_dz_b = n_dz.astype(BF16)
    n_dpre = dot_nt(n_dz_b, r.nw2[...]) * (n_sig * (1.0 + n_pre * (1.0 - n_sig)))
    n_dpre_b = n_dpre.astype(BF16)
    agg_grad = r.agg_grad
    mine = agg_grad.at[at(helper, N)]
    agg_grad[at(helper, N), :] = dot_nt(n_dpre_b, nw1[L:, :]).astype(BF16)
    back_flow = flow(4, others, agg_grad.at[pl.ds(0, (H - 1) * N)])
    for k in range(1, H):
        back_flow.send(mine, mine, in_helper(k))

    own = (core * KINDS + kind_own) * (Y_HI * Y_LO) + y
    node_sums = Reduced(flows, r.n, dims, me, me, z_lo, z_hi, in_group, in_core, in_z_lo, in_z_hi)
    edge_sums = Reduced(flows, r.e, dims, me, own, z_lo, z_hi, in_group, in_core, in_z_lo, in_z_hi)

    bias_axes = (
        (r.bias0, H, helper, in_helper),
        (r.bias1, Y_HI * CORES, plane, in_plane),
        (r.bias2, Z_LO, z_lo, in_z_lo),
        (r.bias3, Z_HI, z_hi, in_z_hi),
    )

    def bias_send(step):
        ref, count, slot_i, device_of = bias_axes[step]
        mine = ref.at[slot_i]
        rest = ref.at[pl.ds(0, count - 1)]
        bias_flow = Flow(flows, r.bias_s.at[step], r.bias_r.at[step], rest, rest)
        for k in range(1, count):
            bias_flow.send(mine, mine, device_of(k))
        return bias_flow

    def bias_sum(step, bias_flow):
        ref, count = bias_axes[step][:2]
        bias_flow.wait()
        total = ref[0]
        for k in range(1, count):
            total += ref[k]
        return total

    node_sums.put(0, dot(node.T, n_dpre_b))
    node_sums.put(L, dot(agg.T, n_dpre_b))
    node_sums.put(2 * L, dot(n_hid.T, n_dz_b))
    node_sums.scatter()
    node_din = g_node + dot_nt(n_dpre_b, nw1[:L, :])

    load_grad.wait()
    gedge, dz_b, dpre_b = r.gedge, r.dz_b, r.dpre_b
    back_flow.wait()

    def edge_back(i, sums):
        rows = at(i, ROWS)
        grad = gedge[rows, :].astype(F32) + dot(hot[rows, LOOK:], agg_grad[...])
        dz = norm_back(grad * r.live[rows, :], normed[rows, :], inv[rows, :])
        second = dz.astype(BF16)
        dz_b[rows, :] = second
        dpre = dot_nt(second, r.ew2[...]) * pre[rows, :]
        dpre_b[rows, :] = dpre.astype(BF16)
        return sums[0] + jnp.sum(dpre, axis=0, keepdims=True), sums[1] + jnp.sum(dz, axis=0, keepdims=True)

    zero = jnp.zeros((1, L), F32)
    e_gb1, e_gb2 = lax.fori_loop(0, NBLK, edge_back, (zero, zero))

    scat = r.scat

    def scatter(i):
        rows = at(i, ROWS)
        scat[rows, :] = dot(hot_t[rows, :], dpre_b[...]).astype(BF16)

    edge_sums.put(3 * L, dot(r.hidden_t[...], dz_b[...]))
    edge_sums.scatter_kind(3, owner)
    edge_sums.put(2 * L, dot(r.edge_t[...], dpre_b[...]))
    edge_sums.scatter_kind(2, owner)
    loop(BAND // ROWS, lambda i: scatter(LOOK // ROWS + i))
    edge_sums.put(L, dot(r.look_t[:, :BAND], scat[LOOK:, :]))
    edge_sums.scatter_kind(1, owner)
    loop(LOOK // ROWS, scatter)
    edge_sums.put(0, dot(r.look_t[...], scat[:LOOK, :]))
    edge_sums.scatter_kind(0, owner)
    node_sums.along_z_lo()

    tiles = (e_gb1, e_gb2, jnp.sum(n_dpre, axis=0, keepdims=True), jnp.sum(n_dz, axis=0, keepdims=True))
    for i, row in enumerate(tiles):
        r.bias0[helper, 2 * i : 2 * i + 1, :] = row[:, :LANES]
        r.bias0[helper, 2 * i + 1 : 2 * i + 2, :] = row[:, LANES:]
    bias_flow = bias_send(0)

    halo_back, halo_in = r.halo_back, r.halo_in
    halo_back[...] = dot_nt(scat[BAND:LOOK, :], r.ew1[:L, :]).astype(BF16)
    upper, lower = pl.ds(0, HALO), pl.ds(HALO, HALO)
    back_down = flow(5, halo_back.at[upper], halo_in.at[upper])
    back_up = flow(6, halo_back.at[lower], halo_in.at[lower])
    back_down.send(halo_back.at[upper], halo_in.at[upper], prev_band)
    back_up.send(halo_back.at[lower], halo_in.at[lower], next_band)

    node_sums.along_z_hi()

    band_grad = r.band_grad
    band_grad[...] = dot_nt(scat[:BAND, :], r.ew1[:L, :]) + dot_nt(scat[LOOK:, :], r.ew1[L : 2 * L, :])

    r.bias1[plane] = bias_sum(0, bias_flow)
    bias_flow = bias_send(1)
    edge_sums.along_z_lo()

    back_down.wait()
    back_up.wait()
    node_out, node_in = r.node_out, r.node_in
    node_out[...] = (band_grad[...] + dot(r.halo_t[...], halo_in[...])).astype(BF16)
    node_flow = flow(7, others, node_in)
    for k in range(1, H):
        to = in_helper(k)
        node_flow.send(node_out.at[at(lax.rem(helper + k, H), N)], node_in.at[pl.ds((k - 1) * N, N)], to)

    r.bias2[z_lo] = bias_sum(1, bias_flow)
    bias_flow = bias_send(2)
    edge_sums.along_z_hi()

    node_sums.gather()

    def edge_grad(i):
        rows = at(i, ROWS)
        din = dot_nt(dpre_b[rows, :], r.ew1[2 * L :, :])
        r.edge_new[rows, :] = ((gedge[rows, :].astype(F32) + din) * r.live[rows, :]).astype(BF16)

    loop(NBLK, edge_grad)
    Local(flows, r.edge_new, r.o_edge, r.load_sem.at[2])

    r.bias3[z_hi] = bias_sum(2, bias_flow)
    bias_flow = bias_send(3)
    edge_sums.gather()

    mate = place(y_hi * CORES + 1 - core, z, helper)
    node_sums.hand_on(mate, [(i * CORES + core) * H for i in range(Y_HI)])
    node_flow.wait()
    total = node_out[at(helper, N), :].astype(F32)
    for k in range(H - 1):
        total += node_in[k * N : (k + 1) * N, :].astype(F32)
    r.o_node[...] = total + node_din
    r.o_bias[...] = bias_sum(3, bias_flow)
    edge_sums.hand_on(mate, [core * (G // CORES)])
    node_sums.handed.wait()
    edge_sums.handed.wait()


class Reduced:
    def __init__(self, flows, refs, dims, me, own, z_lo, z_hi, in_group, in_core, in_z_lo, in_z_hi):
        self.flows, self.refs, self.me, self.own, self.z_lo, self.z_hi = flows, refs, me, own, z_lo, z_hi
        self.in_group, self.in_core, self.in_z_lo, self.in_z_hi = in_group, in_core, in_z_lo, in_z_hi
        self.G = dims.G
        self.piece = refs.out.shape[0] // dims.G
        rest = pl.ds(0, (self.G - 1) * self.piece)
        self.first = self.flow(0, refs.out.at[rest], refs.land.at[rest])

    def flow(self, i, sent, landed):
        return Flow(self.flows, self.refs.s.at[i], self.refs.r.at[i], sent, landed)

    def put(self, first, value):
        out = self.refs.out
        half, count = out.shape[0] // 2, value.shape[0]
        out[first : first + count, :] = value[:, :LANES].astype(BF16)
        out[half + first : half + first + count, :] = value[:, LANES:].astype(BF16)

    def scatter_to(self, g, piece_i, device):
        piece = self.piece
        self.first.send(self.refs.out.at[at(piece_i, piece)], self.refs.land.at[at(self.me, piece)], device)

    def scatter(self):
        for k in range(1, self.G):
            g, to = self.in_group(k)
            self.scatter_to(g, g, to)

    def scatter_kind(self, kind, owner):
        for j in range(self.G // 4):
            g, piece_i, to = owner(kind, j)

            @pl.when(g != self.me)
            def _():
                self.scatter_to(g, piece_i, to)

    def along_z_lo(self):
        out, land, quad, piece = self.refs.out, self.refs.land, self.refs.z_lo, self.piece
        self.first.wait()
        land[at(self.me, piece), :] = out[at(self.own, piece), :]
        zero = jnp.zeros((piece, LANES), F32)
        total = lax.fori_loop(0, self.G, lambda k, acc: acc + land[at(k, piece), :].astype(F32), zero)
        mine = quad.at[self.z_lo]
        quad[self.z_lo] = total.astype(BF16)
        rest = quad.at[pl.ds(0, Z_LO - 1)]
        self.second = self.flow(1, rest, rest)
        for k in range(1, Z_LO):
            self.second.send(mine, mine, self.in_z_lo(k))

    def along_z_hi(self):
        old, quad = self.refs.z_lo, self.refs.z_hi
        self.second.wait()
        total = old[0].astype(F32)
        for k in range(1, Z_LO):
            total += old[k].astype(F32)
        mine = quad.at[self.z_hi]
        quad[self.z_hi] = total.astype(BF16)
        rest = quad.at[pl.ds(0, Z_HI - 1)]
        self.third = self.flow(2, rest, rest)
        for k in range(1, Z_HI):
            self.third.send(mine, mine, self.in_z_hi(k))

    def gather(self):
        quad, full, piece, half = self.refs.z_hi, self.refs.full, self.piece, self.G // 2
        self.third.wait()
        total = quad[0].astype(F32)
        for k in range(1, Z_HI):
            total += quad[k].astype(F32)
        mine = full.at[at(self.own, piece)]
        full[at(self.own, piece), :] = total.astype(BF16)
        rest = full.at[pl.ds(0, (half - 1) * piece)]
        self.done = self.flow(3, rest, rest)
        for k in range(1, half):
            self.done.send(mine, mine, self.in_core(k))

    def hand_on(self, mate, firsts):
        full, half = self.refs.full, self.G // 2
        self.done.wait()
        whole = full.at[pl.ds(0, half * self.piece)]
        self.handed = self.flow(4, whole, whole)
        count = half * self.piece // len(firsts)
        for first in firsts:
            part = full.at[pl.ds(pl.multiple_of(first * self.piece, 16), count)]
            self.handed.send(part, part, mate)


def finish(dims, node_hbm, edge_hbm, node_sums_hbm, edge_sums_hbm, bias_hbm, o_node, o_edge, *rest):
    o_ew1, o_eb1, o_ew2, o_eb2, o_nw1, o_nb1, o_nw2, o_nb2, node_sums, edge_sums, bias, sems = rest
    pairs = (
        (edge_sums_hbm, edge_sums),
        (node_sums_hbm, node_sums),
        (bias_hbm, bias),
        (edge_hbm, o_edge),
        (node_hbm, o_node),
    )
    copies = [pltpu.make_async_copy(src, dst, sems.at[i]) for i, (src, dst) in enumerate(pairs)]
    for copy in copies:
        copy.start()

    def weights(full, targets, scale):
        half, first = full.shape[0] // 2, 0
        for out in targets:
            count = out.shape[0]
            out[:, :LANES] = full[first : first + count, :].astype(F32) * scale
            out[:, LANES:] = full[half + first : half + first + count, :].astype(F32) * scale
            first += count

    copies[0].wait()
    weights(edge_sums, (o_ew1, o_ew2), dims.edge_scale)
    copies[1].wait()
    weights(node_sums, (o_nw1, o_nw2), dims.node_scale)
    copies[2].wait()
    for i, (out, scale) in enumerate(
        ((o_eb1, dims.edge_scale), (o_eb2, dims.edge_scale), (o_nb1, dims.node_scale), (o_nb2, dims.node_scale))
    ):
        out[:, :LANES] = bias[2 * i : 2 * i + 1, :] * scale
        out[:, LANES:] = bias[2 * i + 1 : 2 * i + 2, :] * scale
    copies[3].wait()
    copies[4].wait()


def on_device(
    node_latent,
    edge_latent,
    grad_out_node,
    grad_out_edge,
    senders,
    receivers,
    band_edges,
    halo_list,
    sea_mask,
    edge_w1,
    edge_b1,
    edge_w2,
    edge_b2,
    node_w1,
    node_b1,
    node_w2,
    node_b2,
):
    H = lax.axis_size("helper")
    bands = lax.axis_size("band")
    N, L = node_latent.shape
    E = edge_latent.shape[0]
    HALO = halo_list.shape[1]
    BAND = N * H
    LOOK = BAND + 2 * HALO
    ALL = LOOK + BAND
    G = H * Y_HI * CORES
    dims = SimpleNamespace(
        H=H,
        E=E,
        N=N,
        HALO=HALO,
        L=L,
        G=G,
        edge_scale=1.0 / math.sqrt(E * H * bands),
        node_scale=1.0 / math.sqrt(N * H * bands),
    )
    V, S, ANY = pltpu.VMEM, pltpu.SMEM, pl.ANY
    inputs = dict(
        node=(node_latent, V),
        edge_hbm=(edge_latent, ANY),
        gnode=(grad_out_node, V),
        gedge_hbm=(grad_out_edge, ANY),
        send_ids=(senders.reshape(E // EB, EB), V),
        recv_ids=(receivers.reshape(E // EB, EB), V),
        band_edges=(band_edges, S),
        halo=(halo_list, V),
        sea=(sea_mask.reshape(1, N), V),
        ew1_hbm=(edge_w1, ANY),
        eb1=(edge_b1.reshape(1, L), V),
        ew2_hbm=(edge_w2, ANY),
        eb2=(edge_b2.reshape(1, L), V),
        nw1_hbm=(node_w1, ANY),
        nb1=(node_b1.reshape(1, L), V),
        nw2_hbm=(node_w2, ANY),
        nb2=(node_b2.reshape(1, L), V),
    )
    n_rows, e_rows = 3 * L * (L // LANES), 4 * L * (L // LANES)
    outputs = dict(
        o_node=((N, L), F32, V),
        o_edge=((E, L), BF16, ANY),
        n_full=((n_rows, LANES), BF16, V),
        e_full=((e_rows, LANES), BF16, V),
        o_bias=((8, LANES), F32, V),
    )
    scratch = dict(
        edge=V((E, L), BF16),
        ew1=V((3 * L, L), BF16),
        ew2=V((L, L), BF16),
        nw1=V((2 * L, L), BF16),
        nw2=V((L, L), BF16),
        gedge=V((E, L), BF16),
        edge_new=V((E, L), BF16),
        look=V((LOOK, L), BF16),
        look_t=V((L, LOOK), BF16),
        edge_t=V((L, E), BF16),
        hidden_t=V((L, E), BF16),
        proj=V((ALL, L), BF16),
        hot=V((E, ALL), BF16),
        hot_t=V((ALL, E), BF16),
        halo_t=V((BAND, 2 * HALO), BF16),
        halo_out=V((HALO, L), BF16),
        halo_back=V((2 * HALO, L), BF16),
        halo_in=V((2 * HALO, L), BF16),
        live=V((E, 1), F32),
        pre=V((E, L), F32),
        hidden=V((E, L), BF16),
        normed=V((E, L), F32),
        inv=V((E, 1), F32),
        msg=V((E, L), BF16),
        dz_b=V((E, L), BF16),
        dpre_b=V((E, L), BF16),
        agg_out=V((BAND, L), BF16),
        agg_in=V((BAND - N, L), BF16),
        agg_grad=V((BAND, L), BF16),
        scat=V((ALL, L), BF16),
        band_grad=V((BAND, L), F32),
        node_out=V((BAND, L), BF16),
        node_in=V((BAND - N, L), BF16),
        n_out=V((n_rows, LANES), BF16),
        n_land=V((n_rows, LANES), BF16),
        n_z_lo=V((Z_LO, n_rows // G, LANES), BF16),
        n_z_hi=V((Z_HI, n_rows // G, LANES), BF16),
        e_out=V((e_rows, LANES), BF16),
        e_land=V((e_rows, LANES), BF16),
        e_z_lo=V((Z_LO, e_rows // G, LANES), BF16),
        e_z_hi=V((Z_HI, e_rows // G, LANES), BF16),
        bias0=V((H, 8, LANES), F32),
        bias1=V((Y_HI * CORES, 8, LANES), F32),
        bias2=V((Z_LO, 8, LANES), F32),
        bias3=V((Z_HI, 8, LANES), F32),
    )
    DMA = pltpu.SemaphoreType.DMA
    scratch.update(load_sem=DMA((7,)), s_sem=DMA((8,)), r_sem=DMA((8,)), n_s=DMA((5,)), n_r=DMA((5,)))
    scratch.update(e_s=DMA((5,)), e_r=DMA((5,)), bias_s=DMA((4,)), bias_r=DMA((4,)))
    node, edge, node_sums, edge_sums, bias = pl.pallas_call(
        functools.partial(kernel, dims, list(inputs) + list(outputs) + list(scratch)),
        out_shape=[jax.ShapeDtypeStruct(shape, dtype) for shape, dtype, _ in outputs.values()],
        in_specs=[pl.BlockSpec(memory_space=space) for _, space in inputs.values()],
        out_specs=[pl.BlockSpec(memory_space=space) for _, _, space in outputs.values()],
        scratch_shapes=list(scratch.values()),
        compiler_params=pltpu.CompilerParams(
            collective_id=0, has_side_effects=True, vmem_limit_bytes=VMEM_BYTES
        ),
        name="layer_back",
    )(*[x for x, _ in inputs.values()])
    shapes = [(N, L), (E, L), (3 * L, L), (1, L), (L, L), (1, L), (2 * L, L), (1, L), (L, L), (1, L)]
    out = pl.pallas_call(
        functools.partial(finish, dims),
        out_shape=[jax.ShapeDtypeStruct(shape, BF16 if i == 1 else F32) for i, shape in enumerate(shapes)],
        in_specs=[pl.BlockSpec(memory_space=ANY)] * 5,
        out_specs=[pl.BlockSpec(memory_space=V)] * 10,
        scratch_shapes=[V((n_rows, LANES), BF16), V((e_rows, LANES), BF16), V((8, LANES), F32), DMA((5,))],
        compiler_params=pltpu.CompilerParams(vmem_limit_bytes=VMEM_BYTES),
        name="finish",
    )(node, edge, node_sums, edge_sums, bias)
    return tuple(x.reshape(L) if x.shape[0] == 1 else x for x in out)


def solution(mesh):
    rows = P(("band", "helper"), None)
    flat = P(("band", "helper"))
    in_specs = (rows,) * 4 + (flat, flat, P(), P("band", None), flat) + (P(),) * 8
    out_specs = (rows, rows) + (P(),) * 8
    return jax.shard_map(on_device, mesh=mesh, in_specs=in_specs, out_specs=out_specs, check_vma=False)
```
